128 devices in a mesh: grp: 16 (over y, x), loc: 8 (over z, core).
Axes of the slice: x: 4, y: 4, z: 4, core: 2. Of those that a mesh axis runs over, the one named last changes fastest.
Arguments:
- stream_in: bfloat16 [16384, 3584], P(('grp', 'loc')), may hold values from -6 to 6
- norm_gain: float32 [3584], replicated, may hold values from 0.1 to 1.9
- shared_gate: bfloat16 [3584, 1024], P('grp', 'loc'), may hold values from -0.09375 to 0.09375
- shared_up: bfloat16 [3584, 1024], P('grp', 'loc'), may hold values from -0.09375 to 0.09375
- shared_down: bfloat16 [1024, 3584], P('loc', 'grp'), may hold values from -0.1875 to 0.1875
- expert_gate: bfloat16 [128, 3584, 1024], P(('grp', 'loc')), may hold values from -0.09375 to 0.09375
- expert_up: bfloat16 [128, 3584, 1024], P(('grp', 'loc')), may hold values from -0.09375 to 0.09375
- expert_down: bfloat16 [128, 1024, 3584], P(('grp', 'loc')), may hold values from -0.1875 to 0.1875
- expert_ids: int32 [16384, 8], P(('grp', 'loc')), may hold values from 0 to 127, as said below
- gate_weights: bfloat16 [16384, 8], P(('grp', 'loc')), may hold values from 0.049804688 to 0.5
- cotangent: bfloat16 [16384, 3584], P(('grp', 'loc')), may hold values from -0.100097656 to 0.100097656
Outputs:
- layer_out: bfloat16 [16384, 3584], P(('grp', 'loc'))
- gate_grads: float32 [16384, 8], P(('grp', 'loc'))
The draws below stay inside these ranges and needn't reach their ends.
Inputs may be any that keep to these rules, and one draw needn't show every extreme that they name: `expert_ids`: each token names 8 different experts, two from each of exactly 4 groups, a group being 8 consecutive experts. Among the 128 tokens of one device (aligned blocks of rows), every group is named by exactly 32 tokens and no expert by more than 9; in every group one expert is named by exactly 9 tokens of every device.
All inputs are finite; a program needn't handle non-finite values.
Results may differ from the reference program's by a relative error of at most 0.015.
Values may be sent and summed in bfloat16 or wider, within the bound.
A program may use at most 192 MiB of HBM per device.

```python
import math
import jax
import jax.numpy as jnp
from jax import lax

D = 3584
FF = 1024
FFS = 1024
TOP = 8
TOK_DEV = 128
EXPERTS = 128
SPLITS = 8
TOKENS = 16384
SLOTS = 9
N_GRP = 16
N_LOC = 8


def draw_expert_ids(key, part):
    key = jax.random.fold_in(key, 7)
    subkeys = jax.random.split(key, 4)
    devices = N_GRP * N_LOC
    group_order = jax.vmap(lambda subkey: jax.random.permutation(subkey, N_GRP))(jax.random.split(subkeys[0], devices))
    token_order = jax.vmap(lambda subkey: jax.random.permutation(subkey, TOK_DEV))(jax.random.split(subkeys[1], devices))
    favoured = jax.random.randint(subkeys[2], (N_GRP,), 0, N_LOC)
    others = jax.vmap(lambda subkey: jax.random.permutation(subkey, N_LOC - 1))(jax.random.split(subkeys[3], devices * N_GRP))
    others = others.reshape(devices, N_GRP, N_LOC - 1)
    head_column = jnp.broadcast_to(favoured[None, :, None], (devices, N_GRP, 1))
    ranking = jnp.concatenate([head_column, (favoured[None, :, None] + 1 + others) % N_LOC], axis=2)
    set_index = token_order % 4
    offsets = jnp.arange(4, dtype=jnp.int32)
    order_slot = 4 * set_index[:, :, None] + offsets[None, None, :]
    device_index = jnp.arange(devices, dtype=jnp.int32)[:, None, None]
    chosen_group = group_order[device_index, order_slot % N_GRP]
    within = token_order[:, :, None] // 4 + TOK_DEV // 4 * (order_slot // N_GRP)
    group_rows = 4 * TOK_DEV // N_GRP
    mean_load = 8 * TOK_DEV // devices
    slot_bound = 9 * TOK_DEV // devices

    def pick_lane(position):
        return jnp.where(position < slot_bound, 0, position // mean_load)
    chosen_pair = jnp.stack([pick_lane(within), pick_lane(within + group_rows)], axis=3)
    in_group = ranking[device_index[..., None], chosen_group[..., None], chosen_pair]
    expert = chosen_group[..., None] * N_LOC + in_group
    return expert.reshape(devices * TOK_DEV, 8).astype(jnp.int32)


def levels(own_key, dims, cuts, smallest, top_value):
    def one(dim, blocks):
        draws = jax.random.uniform(jax.random.fold_in(jax.random.fold_in(own_key, 6), dim), (blocks,), jnp.float32, smallest / len(cuts), top_value / len(cuts))
        return jnp.repeat(jnp.exp(draws), dims[dim] // blocks).reshape((-1,) + (1,) * (len(dims) - dim - 1))

    gain = one(*cuts[0])
    for cut in cuts[1:]:
        gain = gain * one(*cut)
    return gain


def centred(own_key, shape, width, most, pieces=(), kind=jnp.bfloat16):
    array = width * jax.random.normal(own_key, shape, jnp.float32)
    if pieces:
        array = array * levels(own_key, shape, pieces, -0.22, 0.18)
    return jnp.clip(array, -most, most).astype(kind)


def setup_inputs(seed: int = 0) -> dict:
    key_list = jax.random.split(jax.random.key(seed), 12)
    stream_in = centred(key_list[0], (TOKENS, D), 1.0, 6.0, ((0, 128),))
    norm_gain = jnp.clip(1.0 + 0.18 * jax.random.normal(key_list[1], (D,), jnp.float32), 0.1, 1.9)
    shared_gate = centred(key_list[2], (D, FFS), D ** -0.5, 0.09375, ((0, 16), (1, 8)))
    shared_up = centred(key_list[3], (D, FFS), D ** -0.5, 0.09375, ((0, 16), (1, 8)))
    shared_down = centred(key_list[4], (FFS, D), FFS ** -0.5, 0.1875, ((0, 8), (1, 16)))
    expert_gate = centred(key_list[5], (EXPERTS, D, FF), D ** -0.5, 0.09375, ((0, 128),))
    expert_up = centred(key_list[6], (EXPERTS, D, FF), D ** -0.5, 0.09375, ((0, 128),))
    expert_down = centred(key_list[7], (EXPERTS, FF, D), FF ** -0.5, 0.1875, ((0, 128),))
    expert_ids = draw_expert_ids(jax.random.fold_in(key_list[11], 71), 0)
    gate_weights = jnp.clip(jnp.exp(math.log(0.5) - 2.306499 * jax.random.uniform(key_list[9], (TOKENS, TOP), jnp.float32) ** levels(key_list[9], (TOKENS, TOP), ((0, 128),), -0.2, 0.2)), 0.049804688, 0.5).astype(jnp.bfloat16)
    cotangent = centred(key_list[10], (TOKENS, D), (D ** -0.5), 0.100097656, ((0, 128),))
    return dict(stream_in=stream_in, norm_gain=norm_gain, shared_gate=shared_gate, shared_up=shared_up, shared_down=shared_down, expert_gate=expert_gate, expert_up=expert_up, expert_down=expert_down, expert_ids=expert_ids, gate_weights=gate_weights, cotangent=cotangent)


epsilon = 1e-06

def swiglu_rows(inputs, w_gate, w_up, w_down):
    gate_act = jnp.dot(inputs, w_gate, preferred_element_type=jnp.float32)
    up_act = jnp.dot(inputs, w_up, preferred_element_type=jnp.float32)
    hidden = (jax.nn.silu(gate_act) * up_act).astype(jnp.bfloat16)
    return jnp.dot(hidden, w_down, preferred_element_type=jnp.float32)

def reference(stream_in, norm_gain, shared_gate, shared_up, shared_down, expert_gate, expert_up, expert_down, expert_ids, gate_weights, cotangent):
    values = stream_in.astype(jnp.float32)
    inverse_rms = lax.rsqrt(lax.optimization_barrier(jnp.mean(values * values, axis=1, keepdims=True)) + epsilon)
    normed = (values * inverse_rms * norm_gain).astype(jnp.bfloat16)
    shared_width = FFS // SPLITS
    shared_out = jnp.zeros((TOKENS, D), jnp.float32)
    for slice_index in range(SPLITS):
        offset = slice_index * shared_width
        partial_term = swiglu_rows(normed, shared_gate[:, offset:offset + shared_width], shared_up[:, offset:offset + shared_width], shared_down[offset:offset + shared_width])
        shared_out = shared_out + lax.optimization_barrier(partial_term.astype(jnp.bfloat16)).astype(jnp.float32)
    flat_ids = expert_ids.reshape(TOKENS * TOP)
    flat_gates = gate_weights.reshape(TOKENS * TOP).astype(jnp.float32)
    pair_token = jnp.arange(TOKENS * TOP, dtype=jnp.int32) // TOP
    capacity = EXPERTS * SLOTS
    cot_f = cotangent.astype(jnp.float32)

    def one_expert(state_pair, expert_index):
        routed, gate_grads = state_pair
        chosen = flat_ids == expert_index
        how_many = jnp.sum(chosen.astype(jnp.int32))
        pair_index = jnp.nonzero(chosen, size=capacity, fill_value=0)[0].astype(jnp.int32)
        filled = jnp.arange(capacity, dtype=jnp.int32) < how_many
        tokens_here = pair_token[pair_index]
        gathered = normed[tokens_here]
        outcome = swiglu_rows(gathered, expert_gate[expert_index], expert_up[expert_index], expert_down[expert_index])
        outcome_f = lax.optimization_barrier(outcome.astype(jnp.bfloat16)).astype(jnp.float32)
        weight = jnp.where(filled, flat_gates[pair_index], 0.0)
        routed = routed.at[tokens_here].add(weight[:, None] * outcome_f)
        products = lax.optimization_barrier(jnp.sum(outcome_f * cot_f[tokens_here], axis=1))
        gate_grads = gate_grads.at[pair_index].add(jnp.where(filled, products, 0.0))
        return ((routed, gate_grads), None)
    start_state = (jnp.zeros((TOKENS, D), jnp.float32), jnp.zeros((TOKENS * TOP,), jnp.float32))
    (routed, gate_grads), _ = lax.scan(one_expert, start_state, jnp.arange(EXPERTS, dtype=jnp.int32))
    layer_out = (shared_out + routed).astype(jnp.bfloat16)
    return (layer_out, gate_grads.reshape(TOKENS, TOP))
```

```python
import functools

import jax
import jax.numpy as jnp
from jax import lax
from jax.experimental import pallas as pl
from jax.experimental.pallas import tpu as pltpu
from jax.sharding import PartitionSpec as P

MESH = pl.DeviceIdType.MESH
F32 = jnp.float32
BF16 = jnp.bfloat16
EPS = 1e-06

D = 3584
FF = 1024
SH = 128
T = 128
GRP, LOC = 16, 8
COL = LOC * T
CAP = 72
W = 512
HALF = W // 2
NS = D // W
PACK = 2 * CAP
SUP = 80
SHARD = D // GRP
ORDER = (
    (0, 1), (0, 3), (1, 0), (3, 0), (1, 1), (3, 3), (1, 3), (3, 1),
    (0, 2), (2, 0), (2, 1), (2, 3), (1, 2), (3, 2), (2, 2),
)
VMEM_LIMIT = 60 * 2**20


def place():
    g, l = lax.axis_index("grp"), lax.axis_index("loc")
    return g, l, l // 2, l % 2


def grp_partner(g, step):
    dy, dx = step
    return ((g // 4 + dy) % 4) * 4 + (g % 4 + dx) % 4


def loc_partner(z, c, dz, dc):
    pz, pc = (z + dz) % 4, (c + dc) % 2
    return pz * 2 + pc, pc * 4 + pz


LOC_STEPS = ((1, 0), (3, 0), (1, 1), (3, 1), (2, 0), (2, 1), (0, 1))


def send(src, dst, send_sem, recv_sem, device):
    copy = pltpu.make_async_remote_copy(
        src_ref=src,
        dst_ref=dst,
        send_sem=send_sem,
        recv_sem=recv_sem,
        device_id=device,
        device_id_type=MESH,
    )
    copy.start()


def drain(ref, sem):
    pltpu.make_async_copy(ref, ref, sem).wait()


def enter(g, l, z, c):
    barrier = pltpu.get_barrier_semaphore()
    for step in ORDER:
        pl.semaphore_signal(
            barrier, inc=1, device_id=(grp_partner(g, step), l), device_id_type=MESH
        )
    for dz, dc in LOC_STEPS:
        pl.semaphore_signal(
            barrier, inc=1, device_id=(g, loc_partner(z, c, dz, dc)[0]), device_id_type=MESH
        )
    return barrier


def dot(a, b):
    return jnp.dot(a, b, preferred_element_type=F32)


def dot_nt(a, b):
    return lax.dot_general(a, b, (((1,), (1,)), ((), ())), preferred_element_type=F32)


def silu(v):
    return v / (1.0 + jnp.exp(-v))


def dispatch_kernel(
    stream, gain, meta, sg, su, cot, wg, wu,
    hidden, shared_hidden, slots, gates, ids_all, cot_all,
    xall, onehot, sbuf, rbuf, accg, accu, wgb, wub, wsh, sacc, meta_all,
    ms, mr, ag_s, ag_r, sib_s, sib_r, cg_s, cg_r, cs_s, cs_r, c_l, d_s, d_r, d_l,
    w_s, w_r, w_l, hbm,
):
    g, l, z, c = place()
    me = c * 4 + z
    barrier = enter(g, l, z, c)
    sibling = loc_partner(z, c, 0, 1)[0]

    def weights(s, slot):
        rows = pl.ds(pl.multiple_of(s * W, W), W)
        return (
            pltpu.make_async_copy(wg.at[0, rows], wgb.at[slot], hbm.at[0, slot]),
            pltpu.make_async_copy(wu.at[0, rows], wub.at[slot], hbm.at[1, slot]),
        )

    for copy in weights(0, 0):
        copy.start()
    meta_all[me] = meta[...]

    def norm_rows(i, carry):
        rows = pl.ds(pl.multiple_of(i * 16, 16), 16)
        v = stream[rows, :].astype(F32)
        scale = lax.rsqrt(jnp.mean(v * v, axis=1, keepdims=True) + EPS)
        n = (v * scale * gain[...]).astype(BF16)
        for s in range(NS):
            xall[s, me, rows, :] = n[:, s * W : (s + 1) * W]
        return carry

    lax.fori_loop(0, T // 16, norm_rows, 0)

    pl.semaphore_wait(barrier, len(ORDER) + len(LOC_STEPS))

    for dz, dc in LOC_STEPS:
        send(meta_all.at[me], meta_all.at[me], ms, mr, (g, loc_partner(z, c, dz, dc)[0]))

    def gather(s, carry):
        for dz in (1, 3, 2):
            send(
                xall.at[s, me], xall.at[s, me], ag_s.at[s], ag_r.at[s],
                (g, loc_partner(z, c, dz, 0)[0]),
            )
        return carry

    lax.fori_loop(0, NS, gather, 0)
    own_rows = pl.ds(pl.multiple_of(g * SHARD, SHARD), SHARD)
    shard_copies = [
        pltpu.make_async_copy(sg, wsh.at[own_rows, 0:SH], w_l.at[0]),
        pltpu.make_async_copy(su, wsh.at[own_rows, SH : 2 * SH], w_l.at[1]),
    ]
    for copy in shard_copies:
        copy.start()

    accg[...] = jnp.zeros_like(accg)
    accu[...] = jnp.zeros_like(accu)
    sacc[...] = jnp.zeros_like(sacc)

    drain(meta_all.at[pl.ds(0, LOC - 1)], mr)
    ids = jnp.concatenate([meta_all[b, 0:8, :] for b in range(LOC)], axis=1)
    gws = jnp.concatenate([meta_all[b, 8:16, :] for b in range(LOC)], axis=1)
    ids_all[...] = ids
    expert = (lax.broadcasted_iota(jnp.int32, (GRP, COL), 0) * LOC + l).astype(F32)
    named = jnp.zeros((GRP, COL), F32)
    gate = jnp.zeros((GRP, COL), F32)
    for k in range(8):
        hit = ids[k : k + 1, :] == expert
        named = named + jnp.where(hit, 1.0, 0.0)
        gate = gate + jnp.where(hit, gws[k : k + 1, :], 0.0)
    before = jnp.where(
        lax.broadcasted_iota(jnp.int32, (T, T), 0) < lax.broadcasted_iota(jnp.int32, (T, T), 1),
        1.0,
        0.0,
    ).astype(BF16)
    ranks = [
        dot(named[:, b * T : (b + 1) * T].astype(BF16), before) + float(b * (CAP // LOC))
        for b in range(LOC)
    ]
    slot = jnp.where(named > 0.5, jnp.concatenate(ranks, axis=1), -100.0)
    slots[...] = slot
    gates[...] = gate
    row = lax.broadcasted_iota(jnp.int32, (CAP, COL), 0).astype(F32)
    for p in range(GRP // 2):
        pair = [jnp.where(row == slot[2 * p + i : 2 * p + i + 1, :], 1.0, 0.0) for i in (0, 1)]
        onehot[pl.ds(PACK * p, PACK), :] = jnp.concatenate(pair, axis=0).astype(BF16)

    def to_sibling(s):
        drain(xall.at[s, pl.ds(0, 3)], ag_r.at[s])
        mine = xall.at[s, pl.ds(c * 4, 4)]
        send(mine, mine, sib_s.at[s], sib_r.at[s], (g, sibling))

    def exchange(s):
        drain(xall.at[s, pl.ds(0, 4)], sib_r.at[s])

        def rows(i, carry):
            x = xall[s].reshape(COL, W)
            o = dot(onehot[pl.ds(pl.multiple_of(i * 4 * CAP, 4 * CAP), 4 * CAP), :], x)
            o = o.reshape(4, CAP, W)
            sbuf[s, pl.ds(i * 4, 4)] = jnp.concatenate(
                [o[:, :, :HALF], o[:, :, HALF:]], axis=1
            ).astype(BF16)
            return carry

        lax.fori_loop(0, GRP // 4, rows, 0)
        for step in ORDER:
            p = grp_partner(g, step)
            send(sbuf.at[s, p], rbuf.at[s, g], d_s.at[s], d_r.at[s], (p, l))
        pltpu.make_async_copy(sbuf.at[s, g], rbuf.at[s, g], d_l.at[s]).start()

    def cot_gather(s):
        cols = cot.at[:, pl.ds(pl.multiple_of(s * W, W), W)]
        pltpu.make_async_copy(cols, cot_all.at[s, me], c_l.at[s]).start()
        for dz in (1, 3, 2):
            send(
                cols, cot_all.at[s, me], cg_s.at[s], cg_r.at[s],
                (g, loc_partner(z, c, dz, 0)[0]),
            )

    def cot_sibling(s):
        drain(cot_all.at[s, pl.ds(0, 3)], cg_r.at[s])
        drain(cot_all.at[s, 0], c_l.at[s])
        mine = cot_all.at[s, pl.ds(c * 4, 4)]
        send(mine, mine, cs_s.at[s], cs_r.at[s], (g, sibling))

    def expert_in(s):
        slot_now = s % 2
        for copy in weights(s, slot_now):
            copy.wait()
        drain(rbuf.at[s, pl.ds(0, GRP - 1)], d_r.at[s])
        drain(rbuf.at[s, 0], d_l.at[s])

        def rows(i, carry):
            xa = rbuf[s, pl.ds(i * 4, 4), 0:SUP, :].reshape(4 * SUP, HALF)
            xb = rbuf[s, pl.ds(i * 4, 4), PACK - SUP : PACK, :].reshape(4 * SUP, HALF)
            for acc, w in ((accg, wgb), (accu, wub)):
                for n in range(2):
                    cols = slice(n * W, (n + 1) * W)
                    a = dot(xa, w[slot_now, 0:HALF, cols]).reshape(4, SUP, W)
                    b = dot(xb, w[slot_now, HALF:W, cols]).reshape(4, SUP, W)
                    acc[pl.ds(i * 4, 4), :, cols] += a[:, 0:CAP] + b[:, SUP - CAP :]
            return carry

        lax.fori_loop(0, GRP // 4, rows, 0)

    to_sibling(0)
    exchange(0)
    to_sibling(1)

    def step(s, carry):
        for copy in weights(s + 1, (s + 1) % 2):
            copy.start()
        exchange(s + 1)

        @pl.when(s + 2 < NS)
        def _():
            to_sibling(s + 2)

        cot_gather(s)

        @pl.when(s > 0)
        def _():
            cot_sibling(s - 1)

        expert_in(s)
        return carry

    def shard_sends(steps):
        for st in steps:
            p = grp_partner(g, st)
            send(sg, wsh.at[own_rows, 0:SH], w_s.at[0], w_r.at[0], (p, l))
            send(su, wsh.at[own_rows, SH : 2 * SH], w_s.at[1], w_r.at[1], (p, l))

    lax.fori_loop(0, 2, step, 0)
    shard_sends(ORDER)
    lax.fori_loop(2, NS - 1, step, 0)
    cot_gather(NS - 1)
    cot_sibling(NS - 2)

    for copy in shard_copies:
        copy.wait()
    drain(wsh.at[pl.ds(0, D - SHARD), 0:SH], w_r.at[0])
    drain(wsh.at[pl.ds(0, D - SHARD), SH : 2 * SH], w_r.at[1])

    def shared_in(s, carry):
        w = wsh[pl.ds(pl.multiple_of(s * W, W), W), :]
        for i in range(2):
            x = xall[s, pl.ds(i * 4, 4)].reshape(COL // 2, W)
            sacc[pl.ds(i * COL // 2, COL // 2), :] += dot(x, w)
        return carry

    lax.fori_loop(0, NS, shared_in, 0)
    shared_hidden[...] = (silu(sacc[:, 0:SH]) * sacc[:, SH : 2 * SH]).astype(BF16)

    cot_sibling(NS - 1)
    expert_in(NS - 1)

    def activate(i, carry):
        h = silu(accg[pl.ds(i * 2, 2)]) * accu[pl.ds(i * 2, 2)]
        hidden[pl.ds(pl.multiple_of(i * PACK, PACK), PACK), :] = h.reshape(PACK, FF).astype(BF16)
        return carry

    lax.fori_loop(0, GRP // 2, activate, 0)

    drain(meta_all.at[pl.ds(0, LOC - 1)], ms)
    drain(wsh.at[pl.ds(0, D - SHARD), 0:SH], w_s.at[0])
    drain(wsh.at[pl.ds(0, D - SHARD), SH : 2 * SH], w_s.at[1])

    def finish(s, carry):
        drain(xall.at[s, pl.ds(0, 3)], ag_s.at[s])
        drain(xall.at[s, pl.ds(0, 4)], sib_s.at[s])
        drain(cot_all.at[s, pl.ds(0, 3)], cg_s.at[s])
        drain(cot_all.at[s, pl.ds(0, 4)], cs_s.at[s])
        drain(cot_all.at[s, pl.ds(0, 4)], cs_r.at[s])
        drain(sbuf.at[s, pl.ds(0, GRP - 1)], d_s.at[s])
        return carry

    lax.fori_loop(0, NS, finish, 0)


def return_kernel(
    hidden, shared_hidden, slots, gates, ids_all, sd, cot_all, wd,
    out, gg,
    cwa, cwb, ohw, slots4, gacc, wdb, cotb, osend, orecv, psend, rrecv, sda, ggs, ggr,
    o_s, o_r, o_l, p_s, p_r, w_s, w_r, w_l, g_s, g_r, hbm, cot_sem,
):
    g, l, z, c = place()
    me = c * 4 + z
    barrier = enter(g, l, z, c)

    def weights(s, slot):
        cols = pl.ds(pl.multiple_of(s * W, W), W)
        return pltpu.make_async_copy(wd.at[0, :, cols], wdb.at[slot], hbm.at[slot])

    def cotangents(s, slot):
        return pltpu.make_async_copy(cot_all.at[s], cotb.at[slot], cot_sem.at[slot])

    weights(0, 0).start()
    weights(1, 1).start()
    cotangents(0, 0).start()
    own_rows = pl.ds(pl.multiple_of(g * SHARD, SHARD), SHARD)
    own_shard = pltpu.make_async_copy(sd, sda.at[own_rows], w_l)
    own_shard.start()

    def expert_out(s):
        slot_now = s % 2
        weights(s, slot_now).wait()

        def rows(i, carry):
            h = hidden[pl.ds(pl.multiple_of(i * 4 * CAP, 4 * CAP), 4 * CAP), :]
            o = dot(h, wdb[slot_now]).reshape(4, CAP, W)
            osend[s, pl.ds(i * 4, 4)] = jnp.concatenate(
                [o[:, :, :HALF], o[:, :, HALF:]], axis=1
            ).astype(BF16)
            return carry

        lax.fori_loop(0, GRP // 4, rows, 0)
        for step in ORDER:
            p = grp_partner(g, step)
            send(osend.at[s, p], orecv.at[s, g], o_s.at[s], o_r.at[s], (p, l))
        pltpu.make_async_copy(osend.at[s, g], orecv.at[s, g], o_l.at[s]).start()

    pl.semaphore_wait(barrier, len(ORDER) + len(LOC_STEPS))
    for step in ORDER:
        send(sd, sda.at[own_rows], w_s, w_r, (grp_partner(g, step), l))
    expert_out(0)

    slot = slots[...]
    gate = gates[...]
    for i in range(4):
        slots4[i] = slot[4 * i : 4 * i + 4, :]
    gacc[...] = jnp.zeros_like(gacc)
    row = lax.broadcasted_iota(jnp.int32, (SUP, COL), 0).astype(F32)
    for cw, shift in ((cwa, 0.0), (cwb, float(SUP - CAP))):
        for e in range(GRP):
            hit = (row - shift) == slot[e : e + 1, :]
            ohw[pl.ds(SUP * e, SUP), :] = jnp.where(hit, gate[e : e + 1, :], 0.0).astype(BF16)
        for j in range(GRP * SUP // T):
            block = ohw[pl.ds(T * j, T), :].astype(F32)
            cw[:, pl.ds(T * j, T)] = block.T.astype(BF16)

    expert_out(1)
    own_shard.wait()
    drain(sda.at[pl.ds(0, D - SHARD)], w_r)

    def combine(s):
        slot_now = s % 2
        drain(orecv.at[s, pl.ds(0, GRP - 1)], o_r.at[s])
        drain(orecv.at[s, 0], o_l.at[s])
        for half in range(2):
            first = 0 if half == 0 else PACK - SUP
            cw = cwa if half == 0 else cwb
            rows_sd = pl.ds(pl.multiple_of(s * W + half * HALF, HALF), HALF)
            cols = slice(half * HALF, (half + 1) * HALF)

            def tokens(i, carry):
                y = orecv[s, :, first : first + SUP, :].reshape(GRP * SUP, HALF)
                rows = pl.ds(pl.multiple_of(i * 256, 256), 256)
                part = dot(cw[rows, :], y) + dot_nt(shared_hidden[rows, :], sda[rows_sd, :])
                psend[s, pl.ds(i * 2, 2), :, cols] = part.reshape(2, T, HALF).astype(BF16)
                return carry

            lax.fori_loop(0, COL // 256, tokens, 0)
        for dz, dc in LOC_STEPS:
            pl_, blk = loc_partner(z, c, dz, dc)
            send(psend.at[s, blk], rrecv.at[s, me], p_s.at[s], p_r.at[s], (g, pl_))
        rrecv[s, me] = psend[s, me]

        cotangents(s, slot_now).wait()
        for half in range(2):
            first = 0 if half == 0 else PACK - SUP
            shift = 0.0 if half == 0 else float(SUP - CAP)
            cols = slice(half * HALF, (half + 1) * HALF)

            def products(i, carry):
                y = orecv[s, pl.ds(i * 4, 4), first : first + SUP, :].reshape(4 * SUP, HALF)
                pos = lax.broadcasted_iota(jnp.int32, (SUP, COL // 2), 0).astype(F32) - shift
                for h in range(2):
                    tok = slice(h * COL // 2, (h + 1) * COL // 2)
                    ct = cotb[slot_now, pl.ds(h * 4, 4), :, cols].reshape(COL // 2, HALF)
                    prod = dot_nt(y, ct).reshape(4, SUP, COL // 2)
                    sl = slots4[i, :, tok]
                    sums = [
                        jnp.sum(
                            jnp.where(pos == sl[e : e + 1, :], prod[e], 0.0), axis=0, keepdims=True
                        )
                        for e in range(4)
                    ]
                    gacc[i, :, tok] += jnp.concatenate(sums, axis=0)
                return carry

            lax.fori_loop(0, GRP // 4, products, 0)

    def total(s):
        drain(rrecv.at[s, pl.ds(0, LOC - 1)], p_r.at[s])
        acc = rrecv[s, 0].astype(F32)
        for b in range(1, LOC):
            acc = acc + rrecv[s, b].astype(F32)
        out[:, pl.ds(pl.multiple_of(s * W, W), W)] = acc.astype(BF16)

    def step(s, carry):
        @pl.when(s + 1 < NS)
        def _():
            cotangents(s + 1, (s + 1) % 2).start()

        @pl.when(s + 2 < NS)
        def _():
            weights(s + 2, s % 2).start()

        combine(s)

        @pl.when(s + 2 < NS)
        def _():
            expert_out(s + 2)

        @pl.when(s > 0)
        def _():
            total(s - 1)

        return carry

    lax.fori_loop(0, NS, step, 0)

    ids = ids_all[...]
    grads = jnp.zeros((8, COL), F32)
    for i in range(4):
        block = gacc[i]
        for j in range(4):
            e = ((4 * i + j) * LOC + l).astype(F32)
            grads = grads + jnp.where(ids == e, block[j : j + 1, :], 0.0)
    for b in range(LOC):
        ggs[b] = grads[:, b * T : (b + 1) * T]
    for dz, dc in LOC_STEPS:
        pl_, blk = loc_partner(z, c, dz, dc)
        send(ggs.at[blk], ggr.at[me], g_s, g_r, (g, pl_))
    ggr[me] = ggs[me]
    total(NS - 1)
    drain(ggr.at[pl.ds(0, LOC - 1)], g_r)
    acc = ggr[0]
    for b in range(1, LOC):
        acc = acc + ggr[b]
    gg[...] = acc

    drain(ggs.at[pl.ds(0, LOC - 1)], g_s)
    drain(sda.at[pl.ds(0, D - SHARD)], w_s)

    def finish(s, carry):
        drain(osend.at[s, pl.ds(0, GRP - 1)], o_s.at[s])
        drain(psend.at[s, pl.ds(0, LOC - 1)], p_s.at[s])
        return carry

    lax.fori_loop(0, NS, finish, 0)


def body(
    stream_in, norm_gain, shared_gate, shared_up, shared_down, expert_gate, expert_up, expert_down,
    expert_ids, gate_weights, cotangent,
):
    vm = pl.BlockSpec(memory_space=pltpu.VMEM)
    hb = pl.BlockSpec(memory_space=pl.ANY)
    dma = pltpu.SemaphoreType.DMA
    meta = jnp.concatenate([expert_ids.T.astype(F32), gate_weights.T.astype(F32)], axis=0)
    hidden, shared_hidden, slots, gates, ids_all, cot_all = pl.pallas_call(
        dispatch_kernel,
        out_shape=(
            jax.ShapeDtypeStruct((GRP * CAP, FF), BF16),
            jax.ShapeDtypeStruct((COL, SH), BF16),
            jax.ShapeDtypeStruct((GRP, COL), F32),
            jax.ShapeDtypeStruct((GRP, COL), F32),
            jax.ShapeDtypeStruct((8, COL), F32),
            jax.ShapeDtypeStruct((NS, LOC, T, W), BF16),
        ),
        in_specs=[vm] * 6 + [hb] * 2,
        out_specs=(vm,) * 5 + (hb,),
        scratch_shapes=[
            pltpu.VMEM((NS, LOC, T, W), BF16),
            pltpu.VMEM((GRP * CAP, COL), BF16),
            pltpu.VMEM((NS, GRP, PACK, HALF), BF16),
            pltpu.VMEM((NS, GRP, PACK, HALF), BF16),
            pltpu.VMEM((GRP, CAP, FF), F32),
            pltpu.VMEM((GRP, CAP, FF), F32),
            pltpu.VMEM((2, W, FF), BF16),
            pltpu.VMEM((2, W, FF), BF16),
            pltpu.VMEM((D, 2 * SH), BF16),
            pltpu.VMEM((COL, 2 * SH), F32),
            pltpu.VMEM((LOC, 16, T), F32),
        ]
        + [dma(()), dma(())]
        + [dma((NS,))] * 12
        + [dma((2,))] * 3
        + [dma((2, 2))],
        compiler_params=pltpu.CompilerParams(
            collective_id=0, has_side_effects=True, vmem_limit_bytes=VMEM_LIMIT
        ),
        name="dispatch",
    )(
        stream_in, norm_gain.reshape(1, D), meta, shared_gate, shared_up, cotangent,
        expert_gate, expert_up,
    )
    out, grads = pl.pallas_call(
        return_kernel,
        out_shape=(
            jax.ShapeDtypeStruct((T, D), BF16),
            jax.ShapeDtypeStruct((8, T), F32),
        ),
        in_specs=[vm] * 6 + [hb] * 2,
        out_specs=(vm, vm),
        scratch_shapes=[
            pltpu.VMEM((COL, GRP * SUP), BF16),
            pltpu.VMEM((COL, GRP * SUP), BF16),
            pltpu.VMEM((GRP * SUP, COL), BF16),
            pltpu.VMEM((4, 4, COL), F32),
            pltpu.VMEM((4, 4, COL), F32),
            pltpu.VMEM((2, FF, W), BF16),
            pltpu.VMEM((2, LOC, T, W), BF16),
            pltpu.VMEM((NS, GRP, PACK, HALF), BF16),
            pltpu.VMEM((NS, GRP, PACK, HALF), BF16),
            pltpu.VMEM((NS, LOC, T, W), BF16),
            pltpu.VMEM((NS, LOC, T, W), BF16),
            pltpu.VMEM((D, SH), BF16),
            pltpu.VMEM((LOC, 8, T), F32),
            pltpu.VMEM((LOC, 8, T), F32),
        ]
        + [dma((NS,))] * 5
        + [dma(())] * 5
        + [dma((2,))] * 2,
        compiler_params=pltpu.CompilerParams(
            collective_id=1, has_side_effects=True, vmem_limit_bytes=VMEM_LIMIT
        ),
        name="give_back",
    )(hidden, shared_hidden, slots, gates, ids_all, shared_down.T, cot_all, expert_down)
    return out, grads.T


def solution(mesh):
    rows = P(("grp", "loc"), None)
    experts = P(("grp", "loc"), None, None)
    return jax.shard_map(
        body,
        mesh=mesh,
        in_specs=(
            rows, P(), P("grp", "loc"), P("grp", "loc"), P("loc", "grp"), experts, experts, experts,
            rows, rows, rows,
        ),
        out_specs=(rows, rows),
        check_vma=False,
    )
```

```python
import functools

import jax
import jax.numpy as jnp
from jax import lax
from jax.experimental import pallas as pl
from jax.experimental.pallas import tpu as pltpu
from jax.sharding import PartitionSpec as P

MESH = pl.DeviceIdType.MESH
F32 = jnp.float32
BF16 = jnp.bfloat16
EPS = 1e-06

D = 3584
FF = 1024
SH = 128
T = 128
GRP, LOC = 16, 8
COL = LOC * T
CAP = 72
W = 512
HALF = W // 2
NS = D // W
PACK = 2 * CAP
SUP = 80
SHARD = D // GRP
ORDER = (
    (0, 1), (0, 3), (1, 0), (3, 0), (1, 1), (3, 3), (1, 3), (3, 1),
    (0, 2), (2, 0), (2, 1), (2, 3), (1, 2), (3, 2), (2, 2),
)
VMEM_LIMIT = 60 * 2**20


def place():
    g, l = lax.axis_index("grp"), lax.axis_index("loc")
    return g, l, l // 2, l % 2


def grp_partner(g, step):
    dy, dx = step
    return ((g // 4 + dy) % 4) * 4 + (g % 4 + dx) % 4


def loc_partner(z, c, dz, dc):
    pz, pc = (z + dz) % 4, (c + dc) % 2
    return pz * 2 + pc, pc * 4 + pz


LOC_STEPS = ((1, 0), (3, 0), (1, 1), (3, 1), (2, 0), (2, 1), (0, 1))


def send(src, dst, send_sem, recv_sem, device):
    copy = pltpu.make_async_remote_copy(
        src_ref=src,
        dst_ref=dst,
        send_sem=send_sem,
        recv_sem=recv_sem,
        device_id=device,
        device_id_type=MESH,
    )
    copy.start()


def drain(ref, sem):
    pltpu.make_async_copy(ref, ref, sem).wait()


def enter(g, l, z, c):
    barrier = pltpu.get_barrier_semaphore()
    for step in ORDER:
        pl.semaphore_signal(
            barrier, inc=1, device_id=(grp_partner(g, step), l), device_id_type=MESH
        )
    for dz, dc in LOC_STEPS:
        pl.semaphore_signal(
            barrier, inc=1, device_id=(g, loc_partner(z, c, dz, dc)[0]), device_id_type=MESH
        )
    return barrier


def dot(a, b):
    return jnp.dot(a, b, preferred_element_type=F32)


def dot_nt(a, b):
    return lax.dot_general(a, b, (((1,), (1,)), ((), ())), preferred_element_type=F32)


def silu(v):
    return v / (1.0 + jnp.exp(-v))


def dispatch_kernel(
    stream, gain, ids_in, gw_in, sg, su, sd, cot, wg, wu,
    hidden, shared_hidden, slots, gates, ids_all, cot_all, sd_all,
    xall, onehot, sbuf, rbuf, accg, accu, wgb, wub, wsh, sacc, meta_all,
    ms, mr, ag_s, ag_r, sib_s, sib_r, cg_s, cg_r, cs_s, cs_r, c_l, d_s, d_r, d_l,
    w_s, w_r, w_l, hbm,
):
    g, l, z, c = place()
    me = c * 4 + z
    barrier = enter(g, l, z, c)
    sibling = loc_partner(z, c, 0, 1)[0]

    def weights(s, slot):
        rows = pl.ds(pl.multiple_of(s * W, W), W)
        return (
            pltpu.make_async_copy(wg.at[0, rows], wgb.at[slot], hbm.at[0, slot]),
            pltpu.make_async_copy(wu.at[0, rows], wub.at[slot], hbm.at[1, slot]),
        )

    for copy in weights(0, 0):
        copy.start()
    meta_all[me, 0:8, :] = ids_in[...].astype(F32)
    meta_all[me, 8:16, :] = gw_in[...].astype(F32)
    row_gain = gain[...].reshape(1, D)

    def norm_rows(i, carry):
        rows = pl.ds(pl.multiple_of(i * 16, 16), 16)
        v = stream[rows, :].astype(F32)
        scale = lax.rsqrt(jnp.mean(v * v, axis=1, keepdims=True) + EPS)
        n = (v * scale * row_gain).astype(BF16)
        for s in range(NS):
            xall[s, me, rows, :] = n[:, s * W : (s + 1) * W]
        return carry

    lax.fori_loop(0, T // 16, norm_rows, 0)

    pl.semaphore_wait(barrier, len(ORDER) + len(LOC_STEPS))

    for dz, dc in LOC_STEPS:
        send(meta_all.at[me], meta_all.at[me], ms, mr, (g, loc_partner(z, c, dz, dc)[0]))

    def gather(s, carry):
        for dz in (1, 3, 2):
            send(
                xall.at[s, me], xall.at[s, me], ag_s.at[s], ag_r.at[s],
                (g, loc_partner(z, c, dz, 0)[0]),
            )
        return carry

    lax.fori_loop(0, NS, gather, 0)
    own_rows = pl.ds(pl.multiple_of(g * SHARD, SHARD), SHARD)
    shard_copies = [
        pltpu.make_async_copy(sg, wsh.at[own_rows, 0:SH], w_l.at[0]),
        pltpu.make_async_copy(su, wsh.at[own_rows, SH : 2 * SH], w_l.at[1]),
        pltpu.make_async_copy(sd, sd_all.at[own_rows], w_l.at[2]),
    ]
    for copy in shard_copies:
        copy.start()
    for st in ORDER:
        p = grp_partner(g, st)
        send(sg, wsh.at[own_rows, 0:SH], w_s.at[0], w_r.at[0], (p, l))
        send(su, wsh.at[own_rows, SH : 2 * SH], w_s.at[1], w_r.at[1], (p, l))

    accg[...] = jnp.zeros_like(accg)
    accu[...] = jnp.zeros_like(accu)
    sacc[...] = jnp.zeros_like(sacc)

    drain(meta_all.at[pl.ds(0, LOC - 1)], mr)
    ids = jnp.concatenate([meta_all[b, 0:8, :] for b in range(LOC)], axis=1)
    gws = jnp.concatenate([meta_all[b, 8:16, :] for b in range(LOC)], axis=1)
    ids_all[...] = ids
    expert = (lax.broadcasted_iota(jnp.int32, (GRP, COL), 0) * LOC + l).astype(F32)
    named = jnp.zeros((GRP, COL), F32)
    gate = jnp.zeros((GRP, COL), F32)
    for k in range(8):
        hit = ids[k : k + 1, :] == expert
        named = named + jnp.where(hit, 1.0, 0.0)
        gate = gate + jnp.where(hit, gws[k : k + 1, :], 0.0)
    before = jnp.where(
        lax.broadcasted_iota(jnp.int32, (T, T), 0) < lax.broadcasted_iota(jnp.int32, (T, T), 1),
        1.0,
        0.0,
    ).astype(BF16)
    ranks = [
        dot(named[:, b * T : (b + 1) * T].astype(BF16), before) + float(b * (CAP // LOC))
        for b in range(LOC)
    ]
    slot = jnp.where(named > 0.5, jnp.concatenate(ranks, axis=1), -100.0)
    slots[...] = slot
    gates[...] = gate
    row = lax.broadcasted_iota(jnp.int32, (CAP, COL), 0).astype(F32)
    for p in range(GRP // 2):
        pair = [jnp.where(row == slot[2 * p + i : 2 * p + i + 1, :], 1.0, 0.0) for i in (0, 1)]
        onehot[pl.ds(PACK * p, PACK), :] = jnp.concatenate(pair, axis=0).astype(BF16)

    def to_sibling(s):
        drain(xall.at[s, pl.ds(0, 3)], ag_r.at[s])
        mine = xall.at[s, pl.ds(c * 4, 4)]
        send(mine, mine, sib_s.at[s], sib_r.at[s], (g, sibling))

    def exchange(s):
        drain(xall.at[s, pl.ds(0, 4)], sib_r.at[s])

        def rows(i, carry):
            x = xall[s].reshape(COL, W)
            o = dot(onehot[pl.ds(pl.multiple_of(i * 4 * CAP, 4 * CAP), 4 * CAP), :], x)
            o = o.reshape(4, CAP, W)
            sbuf[s, pl.ds(i * 4, 4)] = jnp.concatenate(
                [o[:, :, :HALF], o[:, :, HALF:]], axis=1
            ).astype(BF16)
            return carry

        lax.fori_loop(0, GRP // 4, rows, 0)
        for step in ORDER:
            p = grp_partner(g, step)
            send(sbuf.at[s, p], rbuf.at[s, g], d_s.at[s], d_r.at[s], (p, l))
        pltpu.make_async_copy(sbuf.at[s, g], rbuf.at[s, g], d_l.at[s]).start()

    def cot_gather(s):
        cols = cot.at[:, pl.ds(pl.multiple_of(s * W, W), W)]
        pltpu.make_async_copy(cols, cot_all.at[s, me], c_l.at[s]).start()
        for dz in (1, 3, 2):
            send(
                cols, cot_all.at[s, me], cg_s.at[s], cg_r.at[s],
                (g, loc_partner(z, c, dz, 0)[0]),
            )

    def cot_sibling(s):
        drain(cot_all.at[s, pl.ds(0, 3)], cg_r.at[s])
        drain(cot_all.at[s, 0], c_l.at[s])
        mine = cot_all.at[s, pl.ds(c * 4, 4)]
        send(mine, mine, cs_s.at[s], cs_r.at[s], (g, sibling))

    def expert_in(s):
        slot_now = s % 2
        for copy in weights(s, slot_now):
            copy.wait()
        drain(rbuf.at[s, pl.ds(0, GRP - 1)], d_r.at[s])
        drain(rbuf.at[s, 0], d_l.at[s])

        def rows(i, carry):
            xa = rbuf[s, pl.ds(i * 4, 4), 0:SUP, :].reshape(4 * SUP, HALF)
            xb = rbuf[s, pl.ds(i * 4, 4), PACK - SUP : PACK, :].reshape(4 * SUP, HALF)
            for acc, w in ((accg, wgb), (accu, wub)):
                for n in range(2):
                    cols = slice(n * W, (n + 1) * W)
                    a = dot(xa, w[slot_now, 0:HALF, cols]).reshape(4, SUP, W)
                    b = dot(xb, w[slot_now, HALF:W, cols]).reshape(4, SUP, W)
                    acc[pl.ds(i * 4, 4), :, cols] += a[:, 0:CAP] + b[:, SUP - CAP :]
            return carry

        lax.fori_loop(0, GRP // 4, rows, 0)

    to_sibling(0)
    exchange(0)
    to_sibling(1)

    def step(s, carry):
        for copy in weights(s + 1, (s + 1) % 2):
            copy.start()
        exchange(s + 1)

        @pl.when(s + 2 < NS)
        def _():
            to_sibling(s + 2)

        cot_gather(s)

        @pl.when(s > 0)
        def _():
            cot_sibling(s - 1)

        expert_in(s)
        return carry

    lax.fori_loop(0, NS - 1, step, 0)
    for st in ORDER:
        send(sd, sd_all.at[own_rows], w_s.at[2], w_r.at[2], (grp_partner(g, st), l))
    cot_gather(NS - 1)
    cot_sibling(NS - 2)

    for copy in shard_copies:
        copy.wait()
    drain(wsh.at[pl.ds(0, D - SHARD), 0:SH], w_r.at[0])
    drain(wsh.at[pl.ds(0, D - SHARD), SH : 2 * SH], w_r.at[1])

    def shared_in(s, carry):
        w = wsh[pl.ds(pl.multiple_of(s * W, W), W), :]
        for i in range(2):
            x = xall[s, pl.ds(i * 4, 4)].reshape(COL // 2, W)
            sacc[pl.ds(i * COL // 2, COL // 2), :] += dot(x, w)
        return carry

    lax.fori_loop(0, NS, shared_in, 0)
    shared_hidden[...] = (silu(sacc[:, 0:SH]) * sacc[:, SH : 2 * SH]).astype(BF16)

    cot_sibling(NS - 1)
    expert_in(NS - 1)

    def activate(i, carry):
        h = silu(accg[pl.ds(i * 2, 2)]) * accu[pl.ds(i * 2, 2)]
        hidden[pl.ds(pl.multiple_of(i * PACK, PACK), PACK), :] = h.reshape(PACK, FF).astype(BF16)
        return carry

    lax.fori_loop(0, GRP // 2, activate, 0)

    drain(meta_all.at[pl.ds(0, LOC - 1)], ms)
    drain(wsh.at[pl.ds(0, D - SHARD), 0:SH], w_s.at[0])
    drain(wsh.at[pl.ds(0, D - SHARD), SH : 2 * SH], w_s.at[1])
    drain(sd_all.at[pl.ds(0, D - SHARD)], w_s.at[2])
    drain(sd_all.at[pl.ds(0, D - SHARD)], w_r.at[2])

    def finish(s, carry):
        drain(xall.at[s, pl.ds(0, 3)], ag_s.at[s])
        drain(xall.at[s, pl.ds(0, 4)], sib_s.at[s])
        drain(cot_all.at[s, pl.ds(0, 3)], cg_s.at[s])
        drain(cot_all.at[s, pl.ds(0, 4)], cs_s.at[s])
        drain(cot_all.at[s, pl.ds(0, 4)], cs_r.at[s])
        drain(sbuf.at[s, pl.ds(0, GRP - 1)], d_s.at[s])
        return carry

    lax.fori_loop(0, NS, finish, 0)


def return_kernel(
    hidden, shared_hidden, slots, gates, ids_all, cot_all, sd_all, wd,
    out, gg,
    cwa, cwb, ohw, slots4, gacc, wdb, cotb, osend, orecv, psend, rrecv, sda, ggs, ggr,
    o_s, o_r, o_l, p_s, p_r, w_l, g_s, g_r, hbm, cot_sem,
):
    g, l, z, c = place()
    me = c * 4 + z
    barrier = enter(g, l, z, c)

    def weights(s, slot):
        cols = pl.ds(pl.multiple_of(s * W, W), W)
        return pltpu.make_async_copy(wd.at[0, :, cols], wdb.at[slot], hbm.at[slot])

    def cotangents(s, slot):
        return pltpu.make_async_copy(cot_all.at[s], cotb.at[slot], cot_sem.at[slot])

    weights(0, 0).start()
    weights(1, 1).start()
    cotangents(0, 0).start()
    shared_down = pltpu.make_async_copy(sd_all, sda, w_l)
    shared_down.start()

    def expert_out(s):
        slot_now = s % 2
        weights(s, slot_now).wait()

        def rows(i, carry):
            h = hidden[pl.ds(pl.multiple_of(i * 4 * CAP, 4 * CAP), 4 * CAP), :]
            o = dot(h, wdb[slot_now]).reshape(4, CAP, W)
            osend[s, pl.ds(i * 4, 4)] = jnp.concatenate(
                [o[:, :, :HALF], o[:, :, HALF:]], axis=1
            ).astype(BF16)
            return carry

        lax.fori_loop(0, GRP // 4, rows, 0)
        for step in ORDER:
            p = grp_partner(g, step)
            send(osend.at[s, p], orecv.at[s, g], o_s.at[s], o_r.at[s], (p, l))
        pltpu.make_async_copy(osend.at[s, g], orecv.at[s, g], o_l.at[s]).start()

    pl.semaphore_wait(barrier, len(ORDER) + len(LOC_STEPS))
    expert_out(0)

    slot = slots[...]
    gate = gates[...]
    for i in range(4):
        slots4[i] = slot[4 * i : 4 * i + 4, :]
    gacc[...] = jnp.zeros_like(gacc)
    row = lax.broadcasted_iota(jnp.int32, (SUP, COL), 0).astype(F32)
    for cw, shift in ((cwa, 0.0), (cwb, float(SUP - CAP))):
        for e in range(GRP):
            hit = (row - shift) == slot[e : e + 1, :]
            ohw[pl.ds(SUP * e, SUP), :] = jnp.where(hit, gate[e : e + 1, :], 0.0).astype(BF16)
        for j in range(GRP * SUP // T):
            block = ohw[pl.ds(T * j, T), :].astype(F32)
            cw[:, pl.ds(T * j, T)] = block.T.astype(BF16)

    expert_out(1)
    shared_down.wait()

    def combine(s):
        slot_now = s % 2
        drain(orecv.at[s, pl.ds(0, GRP - 1)], o_r.at[s])
        drain(orecv.at[s, 0], o_l.at[s])
        for half in range(2):
            first = 0 if half == 0 else PACK - SUP
            cw = cwa if half == 0 else cwb
            rows_sd = pl.ds(pl.multiple_of(s * W + half * HALF, HALF), HALF)
            cols = slice(half * HALF, (half + 1) * HALF)

            def tokens(i, carry):
                y = orecv[s, :, first : first + SUP, :].reshape(GRP * SUP, HALF)
                rows = pl.ds(pl.multiple_of(i * 256, 256), 256)
                part = dot(cw[rows, :], y) + dot_nt(shared_hidden[rows, :], sda[rows_sd, :])
                psend[s, pl.ds(i * 2, 2), :, cols] = part.reshape(2, T, HALF).astype(BF16)
                return carry

            lax.fori_loop(0, COL // 256, tokens, 0)
            for dz, dc in LOC_STEPS:
                pl_, blk = loc_partner(z, c, dz, dc)
                send(
                    psend.at[s, blk, :, cols], rrecv.at[s, me, :, cols], p_s.at[s], p_r.at[s],
                    (g, pl_),
                )
        rrecv[s, me] = psend[s, me]

        cotangents(s, slot_now).wait()
        for half in range(2):
            first = 0 if half == 0 else PACK - SUP
            shift = 0.0 if half == 0 else float(SUP - CAP)
            cols = slice(half * HALF, (half + 1) * HALF)

            def products(i, carry):
                y = orecv[s, pl.ds(i * 4, 4), first : first + SUP, :].reshape(4 * SUP, HALF)
                pos = lax.broadcasted_iota(jnp.int32, (SUP, COL // 2), 0).astype(F32) - shift
                for h in range(2):
                    tok = slice(h * COL // 2, (h + 1) * COL // 2)
                    ct = cotb[slot_now, pl.ds(h * 4, 4), :, cols].reshape(COL // 2, HALF)
                    prod = dot_nt(y, ct).reshape(4, SUP, COL // 2)
                    sl = slots4[i, :, tok]
                    sums = [
                        jnp.sum(
                            jnp.where(pos == sl[e : e + 1, :], prod[e], 0.0), axis=0, keepdims=True
                        )
                        for e in range(4)
                    ]
                    gacc[i, :, tok] += jnp.concatenate(sums, axis=0)
                return carry

            lax.fori_loop(0, GRP // 4, products, 0)

    def total(s):
        drain(rrecv.at[s, pl.ds(0, LOC - 1)], p_r.at[s])
        acc = rrecv[s, 0].astype(F32)
        for b in range(1, LOC):
            acc = acc + rrecv[s, b].astype(F32)
        out[:, pl.ds(pl.multiple_of(s * W, W), W)] = acc.astype(BF16)

    def step(s, carry):
        @pl.when(s + 1 < NS)
        def _():
            cotangents(s + 1, (s + 1) % 2).start()

        @pl.when(s + 2 < NS)
        def _():
            weights(s + 2, s % 2).start()

        combine(s)

        @pl.when(s + 2 < NS)
        def _():
            expert_out(s + 2)

        @pl.when(s > 0)
        def _():
            total(s - 1)

        return carry

    lax.fori_loop(0, NS, step, 0)

    ids = ids_all[...]
    grads = jnp.zeros((8, COL), F32)
    for i in range(4):
        block = gacc[i]
        for j in range(4):
            e = ((4 * i + j) * LOC + l).astype(F32)
            grads = grads + jnp.where(ids == e, block[j : j + 1, :], 0.0)
    for b in range(LOC):
        ggs[b] = grads[:, b * T : (b + 1) * T]
    for dz, dc in LOC_STEPS:
        pl_, blk = loc_partner(z, c, dz, dc)
        send(ggs.at[blk], ggr.at[me], g_s, g_r, (g, pl_))
    ggr[me] = ggs[me]
    total(NS - 1)
    drain(ggr.at[pl.ds(0, LOC - 1)], g_r)
    acc = ggr[0]
    for b in range(1, LOC):
        acc = acc + ggr[b]
    gg[...] = acc

    drain(ggs.at[pl.ds(0, LOC - 1)], g_s)

    def finish(s, carry):
        drain(osend.at[s, pl.ds(0, GRP - 1)], o_s.at[s])
        drain(psend.at[s, pl.ds(0, LOC - 1)], p_s.at[s])
        return carry

    lax.fori_loop(0, NS, finish, 0)


def body(
    stream_in, norm_gain, shared_gate, shared_up, shared_down, expert_gate, expert_up, expert_down,
    expert_ids, gate_weights, cotangent,
):
    vm = pl.BlockSpec(memory_space=pltpu.VMEM)
    hb = pl.BlockSpec(memory_space=pl.ANY)
    dma = pltpu.SemaphoreType.DMA
    hidden, shared_hidden, slots, gates, ids_all, cot_all, sd_all = pl.pallas_call(
        dispatch_kernel,
        out_shape=(
            jax.ShapeDtypeStruct((GRP * CAP, FF), BF16),
            jax.ShapeDtypeStruct((COL, SH), BF16),
            jax.ShapeDtypeStruct((GRP, COL), F32),
            jax.ShapeDtypeStruct((GRP, COL), F32),
            jax.ShapeDtypeStruct((8, COL), F32),
            jax.ShapeDtypeStruct((NS, LOC, T, W), BF16),
            jax.ShapeDtypeStruct((D, SH), BF16),
        ),
        in_specs=[vm] * 8 + [hb] * 2,
        out_specs=(vm,) * 5 + (hb,) * 2,
        scratch_shapes=[
            pltpu.VMEM((NS, LOC, T, W), BF16),
            pltpu.VMEM((GRP * CAP, COL), BF16),
            pltpu.VMEM((NS, GRP, PACK, HALF), BF16),
            pltpu.VMEM((NS, GRP, PACK, HALF), BF16),
            pltpu.VMEM((GRP, CAP, FF), F32),
            pltpu.VMEM((GRP, CAP, FF), F32),
            pltpu.VMEM((2, W, FF), BF16),
            pltpu.VMEM((2, W, FF), BF16),
            pltpu.VMEM((D, 2 * SH), BF16),
            pltpu.VMEM((COL, 2 * SH), F32),
            pltpu.VMEM((LOC, 16, T), F32),
        ]
        + [dma(()), dma(())]
        + [dma((NS,))] * 12
        + [dma((3,))] * 3
        + [dma((2, 2))],
        compiler_params=pltpu.CompilerParams(
            collective_id=0, has_side_effects=True, vmem_limit_bytes=VMEM_LIMIT
        ),
        name="dispatch",
    )(
        stream_in, norm_gain, expert_ids.T, gate_weights.T, shared_gate, shared_up, shared_down.T,
        cotangent, expert_gate, expert_up,
    )
    out, grads = pl.pallas_call(
        return_kernel,
        out_shape=(
            jax.ShapeDtypeStruct((T, D), BF16),
            jax.ShapeDtypeStruct((8, T), F32),
        ),
        in_specs=[vm] * 5 + [hb] * 3,
        out_specs=(vm, vm),
        scratch_shapes=[
            pltpu.VMEM((COL, GRP * SUP), BF16),
            pltpu.VMEM((COL, GRP * SUP), BF16),
            pltpu.VMEM((GRP * SUP, COL), BF16),
            pltpu.VMEM((4, 4, COL), F32),
            pltpu.VMEM((4, 4, COL), F32),
            pltpu.VMEM((2, FF, W), BF16),
            pltpu.VMEM((2, LOC, T, W), BF16),
            pltpu.VMEM((NS, GRP, PACK, HALF), BF16),
            pltpu.VMEM((NS, GRP, PACK, HALF), BF16),
            pltpu.VMEM((NS, LOC, T, W), BF16),
            pltpu.VMEM((NS, LOC, T, W), BF16),
            pltpu.VMEM((D, SH), BF16),
            pltpu.VMEM((LOC, 8, T), F32),
            pltpu.VMEM((LOC, 8, T), F32),
        ]
        + [dma((NS,))] * 5
        + [dma(())] * 3
        + [dma((2,))] * 2,
        compiler_params=pltpu.CompilerParams(
            collective_id=1, has_side_effects=True, vmem_limit_bytes=VMEM_LIMIT
        ),
        name="give_back",
    )(hidden, shared_hidden, slots, gates, ids_all, cot_all, sd_all, expert_down)
    return out, grads.T


def solution(mesh):
    rows = P(("grp", "loc"), None)
    experts = P(("grp", "loc"), None, None)
    return jax.shard_map(
        body,
        mesh=mesh,
        in_specs=(
            rows, P(), P("grp", "loc"), P("grp", "loc"), P("loc", "grp"), experts, experts, experts,
            rows, rows, rows,
        ),
        out_specs=(rows, rows),
        check_vma=False,
    )
```

```python
import functools

import jax
import jax.numpy as jnp
from jax import lax
from jax.experimental import pallas as pl
from jax.experimental.pallas import tpu as pltpu
from jax.sharding import PartitionSpec as P

MESH = pl.DeviceIdType.MESH
F32 = jnp.float32
BF16 = jnp.bfloat16
EPS = 1e-06

D = 3584
FF = 1024
SH = 128
T = 128
GRP, LOC = 16, 8
COL = LOC * T
CAP = 72
W = 512
HALF = W // 2
NS = D // W
PACK = 2 * CAP
SUP = 80
SHARD = D // GRP
ORDER = (
    (0, 1), (0, 3), (1, 0), (3, 0), (1, 1), (3, 3), (1, 3), (3, 1),
    (0, 2), (2, 0), (2, 1), (2, 3), (1, 2), (3, 2), (2, 2),
)
RING = 4
VMEM_LIMIT = 62 * 2**20


def place():
    g, l = lax.axis_index("grp"), lax.axis_index("loc")
    return g, l, l // 2, l % 2


def grp_partner(g, step):
    dy, dx = step
    return ((g // 4 + dy) % 4) * 4 + (g % 4 + dx) % 4


def loc_partner(z, c, dz, dc):
    pz, pc = (z + dz) % 4, (c + dc) % 2
    return pz * 2 + pc, pc * 4 + pz


LOC_STEPS = ((1, 0), (3, 0), (1, 1), (3, 1), (2, 0), (2, 1), (0, 1))


def send(src, dst, send_sem, recv_sem, device):
    copy = pltpu.make_async_remote_copy(
        src_ref=src,
        dst_ref=dst,
        send_sem=send_sem,
        recv_sem=recv_sem,
        device_id=device,
        device_id_type=MESH,
    )
    copy.start()


def drain(ref, sem):
    pltpu.make_async_copy(ref, ref, sem).wait()


def enter(g, l, z, c):
    barrier = pltpu.get_barrier_semaphore()
    for step in ORDER:
        pl.semaphore_signal(
            barrier, inc=1, device_id=(grp_partner(g, step), l), device_id_type=MESH
        )
    for dz, dc in LOC_STEPS:
        pl.semaphore_signal(
            barrier, inc=1, device_id=(g, loc_partner(z, c, dz, dc)[0]), device_id_type=MESH
        )
    return barrier


def dot(a, b):
    return jnp.dot(a, b, preferred_element_type=F32)


def dot_nt(a, b):
    return lax.dot_general(a, b, (((1,), (1,)), ((), ())), preferred_element_type=F32)


def silu(v):
    return v / (1.0 + jnp.exp(-v))


def layer_kernel(
    stream, gain, ids_in, gw_in, sg, su, sd, cot, wg, wu, wd,
    out, gg, cot_all,
    xall, onehot, sbuf, rbuf, accg, accu, wgb, wub, wsh, sacc, meta_all,
    hidden, shared_hidden, slots, gates, sda, cwa, cwb, slots4, gacc, rrecv, ggs, ggr,
    ms, mr, g_s, g_r, free,
    ag_s, ag_r, sib_s, sib_r, cg_s, cg_r, cs_s, cs_r, c_l, d_s, d_r, d_l,
    o_s, o_r, o_l, p_s, p_r,
    w_s, w_r, w_l, hbm,
):
    g, l, z, c = place()
    me = c * 4 + z
    barrier = enter(g, l, z, c)
    sibling = loc_partner(z, c, 0, 1)[0]

    def weights(s, slot):
        rows = pl.ds(pl.multiple_of(s * W, W), W)
        return (
            pltpu.make_async_copy(wg.at[0, rows], wgb.at[slot], hbm.at[0, slot]),
            pltpu.make_async_copy(wu.at[0, rows], wub.at[slot], hbm.at[1, slot]),
        )

    for copy in weights(0, 0):
        copy.start()
    meta_all[me, 0:8, :] = ids_in[...].astype(F32)
    meta_all[me, 8:16, :] = gw_in[...].astype(F32)
    row_gain = gain[...].reshape(1, D)

    def norm_rows(i, carry):
        rows = pl.ds(pl.multiple_of(i * 16, 16), 16)
        v = stream[rows, :].astype(F32)
        scale = lax.rsqrt(jnp.mean(v * v, axis=1, keepdims=True) + EPS)
        n = (v * scale * row_gain).astype(BF16)
        for s in range(NS):
            xall[s, me, rows, :] = n[:, s * W : (s + 1) * W]
        return carry

    lax.fori_loop(0, T // 16, norm_rows, 0)

    pl.semaphore_wait(barrier, len(ORDER) + len(LOC_STEPS))

    for dz, dc in LOC_STEPS:
        send(meta_all.at[me], meta_all.at[me], ms, mr, (g, loc_partner(z, c, dz, dc)[0]))

    def gather(s, carry):
        for dz in (1, 3, 2):
            send(
                xall.at[s, me], xall.at[s, me], ag_s.at[s], ag_r.at[s],
                (g, loc_partner(z, c, dz, 0)[0]),
            )
        return carry

    lax.fori_loop(0, NS, gather, 0)
    own_rows = pl.ds(pl.multiple_of(g * SHARD, SHARD), SHARD)
    shard_copies = [
        pltpu.make_async_copy(sg, wsh.at[own_rows, 0:SH], w_l.at[0]),
        pltpu.make_async_copy(su, wsh.at[own_rows, SH : 2 * SH], w_l.at[1]),
        pltpu.make_async_copy(sd, sda.at[own_rows], w_l.at[2]),
    ]
    for copy in shard_copies:
        copy.start()
    for d in (1, 3, 2):
        along_x, along_y = (grp_partner(g, (0, d)), l), (grp_partner(g, (d, 0)), l)
        send(sg, wsh.at[own_rows, 0:SH], w_s.at[0], w_r.at[0], along_x)
        send(su, wsh.at[own_rows, SH : 2 * SH], w_s.at[1], w_r.at[1], along_y)

    accg[...] = jnp.zeros_like(accg)
    accu[...] = jnp.zeros_like(accu)
    sacc[...] = jnp.zeros_like(sacc)

    drain(meta_all.at[pl.ds(0, LOC - 1)], mr)
    ids = jnp.concatenate([meta_all[b, 0:8, :] for b in range(LOC)], axis=1)
    gws = jnp.concatenate([meta_all[b, 8:16, :] for b in range(LOC)], axis=1)
    expert = (lax.broadcasted_iota(jnp.int32, (GRP, COL), 0) * LOC + l).astype(F32)
    named = jnp.zeros((GRP, COL), F32)
    gate = jnp.zeros((GRP, COL), F32)
    for k in range(8):
        hit = ids[k : k + 1, :] == expert
        named = named + jnp.where(hit, 1.0, 0.0)
        gate = gate + jnp.where(hit, gws[k : k + 1, :], 0.0)
    before = jnp.where(
        lax.broadcasted_iota(jnp.int32, (T, T), 0) < lax.broadcasted_iota(jnp.int32, (T, T), 1),
        1.0,
        0.0,
    ).astype(BF16)
    ranks = [
        dot(named[:, b * T : (b + 1) * T].astype(BF16), before) + float(b * (CAP // LOC))
        for b in range(LOC)
    ]
    slot = jnp.where(named > 0.5, jnp.concatenate(ranks, axis=1), -100.0)
    slots[...] = slot
    gates[...] = gate
    row = lax.broadcasted_iota(jnp.int32, (CAP, COL), 0).astype(F32)
    for p in range(GRP // 2):
        pair = [jnp.where(row == slot[2 * p + i : 2 * p + i + 1, :], 1.0, 0.0) for i in (0, 1)]
        onehot[pl.ds(PACK * p, PACK), :] = jnp.concatenate(pair, axis=0).astype(BF16)

    def to_sibling(s):
        drain(xall.at[s, pl.ds(0, 3)], ag_r.at[s])
        mine = xall.at[s, pl.ds(c * 4, 4)]
        send(mine, mine, sib_s.at[s], sib_r.at[s], (g, sibling))

    def exchange(s):
        drain(xall.at[s, pl.ds(0, 4)], sib_r.at[s])
        spot = s % RING
        if not isinstance(s, int):

            @pl.when(s >= RING)
            def _():
                drain(sbuf.at[spot, pl.ds(0, GRP - 1)], d_s.at[s - RING])

        def rows(i, carry):
            x = xall[s].reshape(COL, W)
            o = dot(onehot[pl.ds(pl.multiple_of(i * 4 * CAP, 4 * CAP), 4 * CAP), :], x)
            o = o.reshape(4, CAP, W)
            sbuf[spot, pl.ds(i * 4, 4)] = jnp.concatenate(
                [o[:, :, :HALF], o[:, :, HALF:]], axis=1
            ).astype(BF16)
            return carry

        lax.fori_loop(0, GRP // 4, rows, 0)
        for step in ORDER:
            p = grp_partner(g, step)
            send(sbuf.at[spot, p], rbuf.at[s, g], d_s.at[s], d_r.at[s], (p, l))
        pltpu.make_async_copy(sbuf.at[spot, g], rbuf.at[s, g], d_l.at[s]).start()

    def cot_gather(s):
        cols = cot.at[:, pl.ds(pl.multiple_of(s * W, W), W)]
        landing = cot_all.at[s, c, pl.ds(pl.multiple_of(z * T, T), T)]
        pltpu.make_async_copy(cols, landing, c_l.at[s]).start()
        for dz in (1, 3, 2):
            send(
                cols, landing, cg_s.at[s], cg_r.at[s],
                (g, loc_partner(z, c, dz, 0)[0]),
            )

    def cot_sibling(s):
        drain(cot_all.at[s, 0, pl.ds(0, 3 * T)], cg_r.at[s])
        drain(cot_all.at[s, 0, pl.ds(0, T)], c_l.at[s])
        mine = cot_all.at[s, c]
        send(mine, mine, cs_s.at[s], cs_r.at[s], (g, sibling))

    def expert_in(s):
        slot_now = s % 2
        for copy in weights(s, slot_now):
            copy.wait()
        drain(rbuf.at[s, pl.ds(0, GRP - 1)], d_r.at[s])
        drain(rbuf.at[s, 0], d_l.at[s])

        def rows(i, carry):
            xa = rbuf[s, pl.ds(i * 4, 4), 0:SUP, :].reshape(4 * SUP, HALF)
            xb = rbuf[s, pl.ds(i * 4, 4), PACK - SUP : PACK, :].reshape(4 * SUP, HALF)
            for acc, w in ((accg, wgb), (accu, wub)):
                for n in range(2):
                    cols = slice(n * W, (n + 1) * W)
                    a = dot(xa, w[slot_now, 0:HALF, cols]).reshape(4, SUP, W)
                    b = dot(xb, w[slot_now, HALF:W, cols]).reshape(4, SUP, W)
                    acc[pl.ds(i * 4, 4), :, cols] += a[:, 0:CAP] + b[:, SUP - CAP :]
            return carry

        lax.fori_loop(0, GRP // 4, rows, 0)

    def pass_shards():
        for copy in shard_copies:
            copy.wait()
        drain(wsh.at[pl.ds(0, 3 * SHARD), 0:SH], w_r.at[0])
        drain(wsh.at[pl.ds(0, 3 * SHARD), SH : 2 * SH], w_r.at[1])
        line = wsh.at[pl.ds(pl.multiple_of((g // 4) * 4 * SHARD, SHARD), 4 * SHARD), 0:SH]
        for d in (1, 3, 2):
            send(line, line, w_s.at[3], w_r.at[3], (grp_partner(g, (d, 0)), l))
            for y in range(4):
                first = pl.multiple_of((y * 4 + g % 4) * SHARD, SHARD)
                piece = wsh.at[pl.ds(first, SHARD), SH : 2 * SH]
                send(piece, piece, w_s.at[4], w_r.at[4], (grp_partner(g, (0, d)), l))

    to_sibling(0)
    pass_shards()
    exchange(0)
    to_sibling(1)

    def step(s, carry):
        for copy in weights(s + 1, (s + 1) % 2):
            copy.start()
        exchange(s + 1)

        @pl.when(s + 2 < NS)
        def _():
            to_sibling(s + 2)

        cot_gather(s)

        @pl.when(s > 0)
        def _():
            cot_sibling(s - 1)

        expert_in(s)
        return carry

    lax.fori_loop(0, NS - 1, step, 0)
    for st in ORDER:
        send(sd, sda.at[own_rows], w_s.at[2], w_r.at[2], (grp_partner(g, st), l))
    cot_gather(NS - 1)
    cot_sibling(NS - 2)

    drain(wsh.at[pl.ds(0, 12 * SHARD), 0:SH], w_r.at[3])
    drain(wsh.at[pl.ds(0, 12 * SHARD), SH : 2 * SH], w_r.at[4])

    def shared_in(s, carry):
        w = wsh[pl.ds(pl.multiple_of(s * W, W), W), :]
        for i in range(2):
            x = xall[s, pl.ds(i * 4, 4)].reshape(COL // 2, W)
            sacc[pl.ds(i * COL // 2, COL // 2), :] += dot(x, w)
        return carry

    lax.fori_loop(0, NS, shared_in, 0)
    shared_hidden[...] = (silu(sacc[:, 0:SH]) * sacc[:, SH : 2 * SH]).astype(BF16)

    cot_sibling(NS - 1)

    for i in range(4):
        slots4[i] = slot[4 * i : 4 * i + 4, :]
    gacc[...] = jnp.zeros_like(gacc)
    row80 = lax.broadcasted_iota(jnp.int32, (SUP, COL), 0).astype(F32)
    for cw, shift in ((cwa, 0.0), (cwb, float(SUP - CAP))):
        for e in range(GRP):
            hit = (row80 - shift) == slots[e : e + 1, :]
            onehot[pl.ds(SUP * e, SUP), :] = jnp.where(hit, gates[e : e + 1, :], 0.0).astype(BF16)
        for j in range(GRP * SUP // T):
            block = onehot[pl.ds(T * j, T), :].astype(F32)
            cw[:, pl.ds(T * j, T)] = block.T.astype(BF16)

    def back_weights(s):
        cols = pl.ds(pl.multiple_of(s * W, W), W)
        spot = (s + 1) % 2
        return [
            pltpu.make_async_copy(
                wd.at[0, h * W : (h + 1) * W, cols],
                wgb.at[spot, :, h * W : (h + 1) * W],
                hbm.at[0, spot],
            )
            for h in range(2)
        ]

    def cotangents(s):
        spot = (s + 1) % 2
        return [
            pltpu.make_async_copy(
                cot_all.at[s, h], wub.at[spot, :, h * W : (h + 1) * W], hbm.at[1, spot]
            )
            for h in range(2)
        ]

    for copy in back_weights(0):
        copy.start()
    expert_in(NS - 1)
    for st in ORDER:
        pl.semaphore_signal(
            free, inc=1, device_id=(grp_partner(g, st), l), device_id_type=MESH
        )
    for copy in back_weights(1):
        copy.start()

    def activate(i, carry):
        h = silu(accg[pl.ds(i * 2, 2)]) * accu[pl.ds(i * 2, 2)]
        hidden[pl.ds(pl.multiple_of(i * PACK, PACK), PACK), :] = h.reshape(PACK, FF).astype(BF16)
        return carry

    lax.fori_loop(0, GRP // 2, activate, 0)

    drain(meta_all.at[pl.ds(0, LOC - 1)], ms)
    drain(wsh.at[pl.ds(0, 3 * SHARD), 0:SH], w_s.at[0])
    drain(wsh.at[pl.ds(0, 3 * SHARD), SH : 2 * SH], w_s.at[1])
    drain(wsh.at[pl.ds(0, 12 * SHARD), 0:SH], w_s.at[3])
    drain(wsh.at[pl.ds(0, 12 * SHARD), SH : 2 * SH], w_s.at[4])

    def sent(s, carry):
        drain(xall.at[s, pl.ds(0, 3)], ag_s.at[s])
        drain(xall.at[s, pl.ds(0, 4)], sib_s.at[s])
        drain(cot_all.at[s, 0, pl.ds(0, 3 * T)], cg_s.at[s])
        drain(cot_all.at[s, 0], cs_s.at[s])
        drain(cot_all.at[s, 0], cs_r.at[s])
        return carry

    lax.fori_loop(0, NS, sent, 0)
    for s_last in range(NS - RING, NS):
        drain(sbuf.at[s_last % RING, pl.ds(0, GRP - 1)], d_s.at[s_last])
    for copy in cotangents(0):
        copy.start()

    def expert_out(s):
        spot, slot_now = s % RING, (s + 1) % 2
        drain(wgb.at[slot_now], hbm.at[0, slot_now])
        if not isinstance(s, int):

            @pl.when(s >= RING)
            def _():
                drain(sbuf.at[spot, pl.ds(0, GRP - 1)], o_s.at[s - RING])

        def rows(i, carry):
            r = pl.ds(pl.multiple_of(i * 4 * CAP, 4 * CAP), 4 * CAP)
            o = dot(hidden[r, 0:W], wgb[slot_now, :, 0:W])
            o = o + dot(hidden[r, W : 2 * W], wgb[slot_now, :, W : 2 * W])
            o = o.reshape(4, CAP, W)
            sbuf[spot, pl.ds(i * 4, 4)] = jnp.concatenate(
                [o[:, :, :HALF], o[:, :, HALF:]], axis=1
            ).astype(BF16)
            return carry

        lax.fori_loop(0, GRP // 4, rows, 0)
        if isinstance(s, int) and s == 0:
            pl.semaphore_wait(free, len(ORDER))
        for st in ORDER:
            p = grp_partner(g, st)
            send(sbuf.at[spot, p], rbuf.at[s, g], o_s.at[s], o_r.at[s], (p, l))
        pltpu.make_async_copy(sbuf.at[spot, g], rbuf.at[s, g], o_l.at[s]).start()

    expert_out(0)
    expert_out(1)
    drain(sda.at[pl.ds(0, D - SHARD)], w_r.at[2])
    drain(sda.at[pl.ds(0, D - SHARD)], w_s.at[2])

    def combine(s):
        slot_now = (s + 1) % 2
        drain(rbuf.at[s, pl.ds(0, GRP - 1)], o_r.at[s])
        drain(rbuf.at[s, 0], o_l.at[s])
        for half in range(2):
            first = 0 if half == 0 else PACK - SUP
            cw = cwa if half == 0 else cwb
            rows_sd = pl.ds(pl.multiple_of(s * W + half * HALF, HALF), HALF)
            cols = slice(half * HALF, (half + 1) * HALF)

            def tokens(i, carry):
                y = rbuf[s, :, first : first + SUP, :].reshape(GRP * SUP, HALF)
                rows = pl.ds(pl.multiple_of(i * 256, 256), 256)
                part = dot(cw[rows, :], y) + dot_nt(shared_hidden[rows, :], sda[rows_sd, :])
                xall[s, pl.ds(i * 2, 2), :, cols] = part.reshape(2, T, HALF).astype(BF16)
                return carry

            lax.fori_loop(0, COL // 256, tokens, 0)
            for dz, dc in LOC_STEPS:
                pl_, blk = loc_partner(z, c, dz, dc)
                send(
                    xall.at[s, blk, :, cols], rrecv.at[s, me, :, cols], p_s.at[s], p_r.at[s],
                    (g, pl_),
                )
        rrecv[s, me] = xall[s, me]

        drain(wub.at[slot_now], hbm.at[1, slot_now])
        for half in range(2):
            first = 0 if half == 0 else PACK - SUP
            shift = 0.0 if half == 0 else float(SUP - CAP)
            cols = slice(half * HALF, (half + 1) * HALF)

            def products(i, carry):
                y = rbuf[s, pl.ds(i * 4, 4), first : first + SUP, :].reshape(4 * SUP, HALF)
                pos = lax.broadcasted_iota(jnp.int32, (SUP, COL // 2), 0).astype(F32) - shift
                for h in range(2):
                    tok = slice(h * COL // 2, (h + 1) * COL // 2)
                    ct = wub[slot_now, :, h * W + half * HALF : h * W + (half + 1) * HALF]
                    prod = dot_nt(y, ct).reshape(4, SUP, COL // 2)
                    sl = slots4[i, :, tok]
                    sums = [
                        jnp.sum(
                            jnp.where(pos == sl[e : e + 1, :], prod[e], 0.0), axis=0, keepdims=True
                        )
                        for e in range(4)
                    ]
                    gacc[i, :, tok] += jnp.concatenate(sums, axis=0)
                return carry

            lax.fori_loop(0, GRP // 4, products, 0)

    def total(s):
        drain(rrecv.at[s, pl.ds(0, LOC - 1)], p_r.at[s])
        acc = rrecv[s, 0].astype(F32)
        for b in range(1, LOC):
            acc = acc + rrecv[s, b].astype(F32)
        out[:, pl.ds(pl.multiple_of(s * W, W), W)] = acc.astype(BF16)

    def back_step(s, carry):
        @pl.when(s + 1 < NS)
        def _():
            for copy in cotangents(s + 1):
                copy.start()

        @pl.when(s + 2 < NS)
        def _():
            for copy in back_weights(s + 2):
                copy.start()

        combine(s)

        @pl.when(s + 2 < NS)
        def _():
            expert_out(s + 2)

        @pl.when(s > 0)
        def _():
            total(s - 1)

        return carry

    lax.fori_loop(0, NS, back_step, 0)

    grads = jnp.zeros((8, COL), F32)
    for i in range(4):
        block = gacc[i]
        for j in range(4):
            e = ((4 * i + j) * LOC + l).astype(F32)
            grads = grads + jnp.where(ids == e, block[j : j + 1, :], 0.0)
    for b in range(LOC):
        ggs[b] = grads[:, b * T : (b + 1) * T]
    for dz, dc in LOC_STEPS:
        pl_, blk = loc_partner(z, c, dz, dc)
        send(ggs.at[blk], ggr.at[me], g_s, g_r, (g, pl_))
    ggr[me] = ggs[me]
    total(NS - 1)
    drain(ggr.at[pl.ds(0, LOC - 1)], g_r)
    acc = ggr[0]
    for b in range(1, LOC):
        acc = acc + ggr[b]
    gg[...] = acc

    drain(ggs.at[pl.ds(0, LOC - 1)], g_s)

    def finish(s, carry):
        drain(xall.at[s, pl.ds(0, LOC - 1)], p_s.at[s])
        return carry

    lax.fori_loop(0, NS, finish, 0)
    for s_last in range(NS - RING, NS):
        drain(sbuf.at[s_last % RING, pl.ds(0, GRP - 1)], o_s.at[s_last])


def body(
    stream_in, norm_gain, shared_gate, shared_up, shared_down, expert_gate, expert_up, expert_down,
    expert_ids, gate_weights, cotangent,
):
    vm = pl.BlockSpec(memory_space=pltpu.VMEM)
    hb = pl.BlockSpec(memory_space=pl.ANY)
    dma = pltpu.SemaphoreType.DMA
    out, grads, _ = pl.pallas_call(
        layer_kernel,
        out_shape=(
            jax.ShapeDtypeStruct((T, D), BF16),
            jax.ShapeDtypeStruct((8, T), F32),
            jax.ShapeDtypeStruct((NS, 2, COL // 2, W), BF16),
        ),
        in_specs=[vm] * 8 + [hb] * 3,
        out_specs=(vm, vm, hb),
        scratch_shapes=[
            pltpu.VMEM((NS, LOC, T, W), BF16),
            pltpu.VMEM((GRP * SUP, COL), BF16),
            pltpu.VMEM((RING, GRP, PACK, HALF), BF16),
            pltpu.VMEM((NS, GRP, PACK, HALF), BF16),
            pltpu.VMEM((GRP, CAP, FF), F32),
            pltpu.VMEM((GRP, CAP, FF), F32),
            pltpu.VMEM((2, W, FF), BF16),
            pltpu.VMEM((2, W, FF), BF16),
            pltpu.VMEM((D, 2 * SH), BF16),
            pltpu.VMEM((COL, 2 * SH), F32),
            pltpu.VMEM((LOC, 16, T), F32),
            pltpu.VMEM((GRP * CAP, FF), BF16),
            pltpu.VMEM((COL, SH), BF16),
            pltpu.VMEM((GRP, COL), F32),
            pltpu.VMEM((GRP, COL), F32),
            pltpu.VMEM((D, SH), BF16),
            pltpu.VMEM((COL, GRP * SUP), BF16),
            pltpu.VMEM((COL, GRP * SUP), BF16),
            pltpu.VMEM((4, 4, COL), F32),
            pltpu.VMEM((4, 4, COL), F32),
            pltpu.VMEM((NS, LOC, T, W), BF16),
            pltpu.VMEM((LOC, 8, T), F32),
            pltpu.VMEM((LOC, 8, T), F32),
        ]
        + [dma(())] * 4
        + [pltpu.SemaphoreType.REGULAR]
        + [dma((NS,))] * 17
        + [dma((5,))] * 2
        + [dma((3,))]
        + [dma((2, 2))],
        compiler_params=pltpu.CompilerParams(
            collective_id=0, has_side_effects=True, vmem_limit_bytes=VMEM_LIMIT
        ),
        name="layer",
    )(
        stream_in, norm_gain, expert_ids.T, gate_weights.T, shared_gate, shared_up, shared_down.T,
        cotangent, expert_gate, expert_up, expert_down,
    )
    return out, grads.T


def solution(mesh):
    rows = P(("grp", "loc"), None)
    experts = P(("grp", "loc"), None, None)
    return jax.shard_map(
        body,
        mesh=mesh,
        in_specs=(
            rows, P(), P("grp", "loc"), P("grp", "loc"), P("loc", "grp"), experts, experts, experts,
            rows, rows, rows,
        ),
        out_specs=(rows, rows),
        check_vma=False,
    )
```

```python
import functools

import jax
import jax.numpy as jnp
from jax import lax
from jax.experimental import pallas as pl
from jax.experimental.pallas import tpu as pltpu
from jax.sharding import PartitionSpec as P

MESH = pl.DeviceIdType.MESH
F32 = jnp.float32
BF16 = jnp.bfloat16
EPS = 1e-06

D = 3584
FF = 1024
SH = 128
T = 128
GRP, LOC = 16, 8
COL = LOC * T
CAP = 72
W = 512
HALF = W // 2
NS = D // W
PACK = 2 * CAP
SUP = 80
SHARD = D // GRP
ORDER = (
    (0, 1), (0, 3), (1, 0), (3, 0), (1, 1), (3, 3), (1, 3), (3, 1),
    (0, 2), (2, 0), (2, 1), (2, 3), (1, 2), (3, 2), (2, 2),
)
RING = 4
VMEM_LIMIT = 62 * 2**20


def place():
    g, l = lax.axis_index("grp"), lax.axis_index("loc")
    return g, l, l // 2, l % 2


def grp_partner(g, step):
    dy, dx = step
    return ((g // 4 + dy) % 4) * 4 + (g % 4 + dx) % 4


def loc_partner(z, c, dz, dc):
    pz, pc = (z + dz) % 4, (c + dc) % 2
    return pz * 2 + pc, pc * 4 + pz


LOC_STEPS = ((1, 0), (3, 0), (1, 1), (3, 1), (2, 0), (2, 1), (0, 1))


def send(src, dst, send_sem, recv_sem, device):
    copy = pltpu.make_async_remote_copy(
        src_ref=src,
        dst_ref=dst,
        send_sem=send_sem,
        recv_sem=recv_sem,
        device_id=device,
        device_id_type=MESH,
    )
    copy.start()


def drain(ref, sem):
    pltpu.make_async_copy(ref, ref, sem).wait()


def enter(g, l, z, c):
    barrier = pltpu.get_barrier_semaphore()
    for step in ORDER:
        pl.semaphore_signal(
            barrier, inc=1, device_id=(grp_partner(g, step), l), device_id_type=MESH
        )
    for dz, dc in LOC_STEPS:
        pl.semaphore_signal(
            barrier, inc=1, device_id=(g, loc_partner(z, c, dz, dc)[0]), device_id_type=MESH
        )
    return barrier


def dot(a, b):
    return jnp.dot(a, b, preferred_element_type=F32)


def dot_nt(a, b):
    return lax.dot_general(a, b, (((1,), (1,)), ((), ())), preferred_element_type=F32)


def silu(v):
    return v / (1.0 + jnp.exp(-v))


def layer_kernel(
    stream, gain, ids_in, gw_in, sg, su, sd, cot, wg, wu, wd,
    out, gg, cot_all,
    xall, onehot, sbuf, rbuf, accg, accu, wgb, wub, wsh, sacc, meta_all,
    hidden, shared_hidden, slots, gates, sda, cwa, cwb, slots4, gacc, rrecv, ggs, ggr,
    ms, mr, g_s, g_r, free,
    ag_s, ag_r, sib_s, sib_r, cg_s, cg_r, cs_s, cs_r, c_l, d_s, d_r, d_l,
    o_s, o_r, o_l, p_s, p_r,
    w_s, w_r, w_l, hbm,
):
    g, l, z, c = place()
    me = c * 4 + z
    barrier = enter(g, l, z, c)
    sibling = loc_partner(z, c, 0, 1)[0]

    def weights(s, slot):
        rows = pl.ds(pl.multiple_of(s * W, W), W)
        return (
            pltpu.make_async_copy(wg.at[0, rows], wgb.at[slot], hbm.at[0, slot]),
            pltpu.make_async_copy(wu.at[0, rows], wub.at[slot], hbm.at[1, slot]),
        )

    for copy in weights(0, 0):
        copy.start()
    meta_all[me, 0:8, :] = ids_in[...].astype(F32)
    meta_all[me, 8:16, :] = gw_in[...].astype(F32)
    row_gain = gain[...].reshape(1, D)

    def norm_rows(i, carry):
        rows = pl.ds(pl.multiple_of(i * 16, 16), 16)
        v = stream[rows, :].astype(F32)
        scale = lax.rsqrt(jnp.mean(v * v, axis=1, keepdims=True) + EPS)
        n = (v * scale * row_gain).astype(BF16)
        for s in range(NS):
            xall[s, me, rows, :] = n[:, s * W : (s + 1) * W]
        return carry

    lax.fori_loop(0, T // 16, norm_rows, 0)

    pl.semaphore_wait(barrier, len(ORDER) + len(LOC_STEPS))

    for dz, dc in LOC_STEPS:
        send(meta_all.at[me], meta_all.at[me], ms, mr, (g, loc_partner(z, c, dz, dc)[0]))

    def gather(s, carry):
        for dz in (1, 3, 2):
            send(
                xall.at[s, me], xall.at[s, me], ag_s.at[s], ag_r.at[s],
                (g, loc_partner(z, c, dz, 0)[0]),
            )
        return carry

    lax.fori_loop(0, NS, gather, 0)
    own_rows = pl.ds(pl.multiple_of(g * SHARD, SHARD), SHARD)
    shard_copies = [
        pltpu.make_async_copy(sg, wsh.at[own_rows, 0:SH], w_l.at[0]),
        pltpu.make_async_copy(su, wsh.at[own_rows, SH : 2 * SH], w_l.at[1]),
        pltpu.make_async_copy(sd, sda.at[own_rows], w_l.at[2]),
    ]
    for copy in shard_copies:
        copy.start()
    for d in (1, 3, 2):
        along_x, along_y = (grp_partner(g, (0, d)), l), (grp_partner(g, (d, 0)), l)
        send(sg, wsh.at[own_rows, 0:SH], w_s.at[0], w_r.at[0], along_x)
        send(su, wsh.at[own_rows, SH : 2 * SH], w_s.at[1], w_r.at[1], along_y)

    accg[...] = jnp.zeros_like(accg)
    accu[...] = jnp.zeros_like(accu)
    sacc[...] = jnp.zeros_like(sacc)

    drain(meta_all.at[pl.ds(0, LOC - 1)], mr)
    ids = jnp.concatenate([meta_all[b, 0:8, :] for b in range(LOC)], axis=1)
    gws = jnp.concatenate([meta_all[b, 8:16, :] for b in range(LOC)], axis=1)
    expert = (lax.broadcasted_iota(jnp.int32, (GRP, COL), 0) * LOC + l).astype(F32)
    named = jnp.zeros((GRP, COL), F32)
    gate = jnp.zeros((GRP, COL), F32)
    for k in range(8):
        hit = ids[k : k + 1, :] == expert
        named = named + jnp.where(hit, 1.0, 0.0)
        gate = gate + jnp.where(hit, gws[k : k + 1, :], 0.0)
    before = jnp.where(
        lax.broadcasted_iota(jnp.int32, (T, T), 0) < lax.broadcasted_iota(jnp.int32, (T, T), 1),
        1.0,
        0.0,
    ).astype(BF16)
    ranks = [
        dot(named[:, b * T : (b + 1) * T].astype(BF16), before) + float(b * (CAP // LOC))
        for b in range(LOC)
    ]
    slot = jnp.where(named > 0.5, jnp.concatenate(ranks, axis=1), -100.0)
    slots[...] = slot
    gates[...] = gate
    row = lax.broadcasted_iota(jnp.int32, (CAP, COL), 0).astype(F32)
    for p in range(GRP // 2):
        pair = [jnp.where(row == slot[2 * p + i : 2 * p + i + 1, :], 1.0, 0.0) for i in (0, 1)]
        onehot[pl.ds(PACK * p, PACK), :] = jnp.concatenate(pair, axis=0).astype(BF16)

    def to_sibling(s):
        drain(xall.at[s, pl.ds(0, 3)], ag_r.at[s])
        mine = xall.at[s, pl.ds(c * 4, 4)]
        send(mine, mine, sib_s.at[s], sib_r.at[s], (g, sibling))

    def exchange(s):
        drain(xall.at[s, pl.ds(0, 4)], sib_r.at[s])
        spot = s % RING
        if not isinstance(s, int):

            @pl.when(s >= RING)
            def _():
                drain(sbuf.at[spot, pl.ds(0, GRP - 1)], d_s.at[s - RING])

        def rows(i, carry):
            x = xall[s].reshape(COL, W)
            o = dot(onehot[pl.ds(pl.multiple_of(i * 4 * CAP, 4 * CAP), 4 * CAP), :], x)
            o = o.reshape(4, CAP, W)
            sbuf[spot, pl.ds(i * 4, 4)] = jnp.concatenate(
                [o[:, :, :HALF], o[:, :, HALF:]], axis=1
            ).astype(BF16)
            return carry

        lax.fori_loop(0, GRP // 4, rows, 0)
        for step in ORDER:
            p = grp_partner(g, step)
            send(sbuf.at[spot, p], rbuf.at[s, g], d_s.at[s], d_r.at[s], (p, l))
        pltpu.make_async_copy(sbuf.at[spot, g], rbuf.at[s, g], d_l.at[s]).start()

    def cot_gather(s):
        cols = cot.at[:, pl.ds(pl.multiple_of(s * W, W), W)]
        landing = cot_all.at[s, c, pl.ds(pl.multiple_of(z * T, T), T)]
        pltpu.make_async_copy(cols, landing, c_l.at[s]).start()
        for dz in (1, 3, 2):
            send(
                cols, landing, cg_s.at[s], cg_r.at[s],
                (g, loc_partner(z, c, dz, 0)[0]),
            )

    def cot_sibling(s):
        drain(cot_all.at[s, 0, pl.ds(0, 3 * T)], cg_r.at[s])
        drain(cot_all.at[s, 0, pl.ds(0, T)], c_l.at[s])
        mine = cot_all.at[s, c]
        send(mine, mine, cs_s.at[s], cs_r.at[s], (g, sibling))

    def expert_in(s):
        slot_now = s % 2
        for copy in weights(s, slot_now):
            copy.wait()
        drain(rbuf.at[s, pl.ds(0, GRP - 1)], d_r.at[s])
        drain(rbuf.at[s, 0], d_l.at[s])

        def rows(i, carry):
            xa = rbuf[s, pl.ds(i * 4, 4), 0:SUP, :].reshape(4 * SUP, HALF)
            xb = rbuf[s, pl.ds(i * 4, 4), PACK - SUP : PACK, :].reshape(4 * SUP, HALF)
            for acc, w in ((accg, wgb), (accu, wub)):
                for n in range(2):
                    cols = slice(n * W, (n + 1) * W)
                    a = dot(xa, w[slot_now, 0:HALF, cols]).reshape(4, SUP, W)
                    b = dot(xb, w[slot_now, HALF:W, cols]).reshape(4, SUP, W)
                    acc[pl.ds(i * 4, 4), :, cols] += a[:, 0:CAP] + b[:, SUP - CAP :]
            return carry

        lax.fori_loop(0, GRP // 4, rows, 0)

    def pass_shards():
        for copy in shard_copies:
            copy.wait()
        drain(wsh.at[pl.ds(0, 3 * SHARD), 0:SH], w_r.at[0])
        drain(wsh.at[pl.ds(0, 3 * SHARD), SH : 2 * SH], w_r.at[1])
        line = wsh.at[pl.ds(pl.multiple_of((g // 4) * 4 * SHARD, SHARD), 4 * SHARD), 0:SH]
        for d in (1, 3, 2):
            send(line, line, w_s.at[3], w_r.at[3], (grp_partner(g, (d, 0)), l))
            for y in range(4):
                first = pl.multiple_of((y * 4 + g % 4) * SHARD, SHARD)
                piece = wsh.at[pl.ds(first, SHARD), SH : 2 * SH]
                send(piece, piece, w_s.at[4], w_r.at[4], (grp_partner(g, (0, d)), l))

    to_sibling(0)
    pass_shards()
    exchange(0)
    to_sibling(1)

    def step(s, carry):
        for copy in weights(s + 1, (s + 1) % 2):
            copy.start()
        exchange(s + 1)

        @pl.when(s + 2 < NS)
        def _():
            to_sibling(s + 2)

        cot_gather(s)

        @pl.when(s > 0)
        def _():
            cot_sibling(s - 1)

        expert_in(s)
        return carry

    lax.fori_loop(0, NS - 1, step, 0)
    for st in ORDER:
        send(sd, sda.at[own_rows], w_s.at[2], w_r.at[2], (grp_partner(g, st), l))
    cot_gather(NS - 1)
    cot_sibling(NS - 2)

    drain(wsh.at[pl.ds(0, 12 * SHARD), 0:SH], w_r.at[3])
    drain(wsh.at[pl.ds(0, 12 * SHARD), SH : 2 * SH], w_r.at[4])

    def shared_in(s, carry):
        w = wsh[pl.ds(pl.multiple_of(s * W, W), W), :]
        for i in range(2):
            x = xall[s, pl.ds(i * 4, 4)].reshape(COL // 2, W)
            sacc[pl.ds(i * COL // 2, COL // 2), :] += dot(x, w)
        return carry

    lax.fori_loop(0, NS, shared_in, 0)
    shared_hidden[...] = (silu(sacc[:, 0:SH]) * sacc[:, SH : 2 * SH]).astype(BF16)

    cot_sibling(NS - 1)

    for i in range(4):
        slots4[i] = slot[4 * i : 4 * i + 4, :]
    gacc[...] = jnp.zeros_like(gacc)
    row80 = lax.broadcasted_iota(jnp.int32, (SUP, COL), 0).astype(F32)
    for cw, shift in ((cwa, 0.0), (cwb, float(SUP - CAP))):
        for e in range(GRP):
            hit = (row80 - shift) == slots[e : e + 1, :]
            onehot[pl.ds(SUP * e, SUP), :] = jnp.where(hit, gates[e : e + 1, :], 0.0).astype(BF16)
        for j in range(GRP * SUP // T):
            block = onehot[pl.ds(T * j, T), :].astype(F32)
            cw[:, pl.ds(T * j, T)] = block.T.astype(BF16)

    def back_weights(s):
        cols = pl.ds(pl.multiple_of(s * W, W), W)
        spot = (s + 1) % 2
        return [
            pltpu.make_async_copy(
                wd.at[0, h * W : (h + 1) * W, cols],
                wgb.at[spot, :, h * W : (h + 1) * W],
                hbm.at[0, spot],
            )
            for h in range(2)
        ]

    def cotangents(s):
        spot = (s + 1) % 2
        return [
            pltpu.make_async_copy(
                cot_all.at[s, h], wub.at[spot, :, h * W : (h + 1) * W], hbm.at[1, spot]
            )
            for h in range(2)
        ]

    for copy in back_weights(0):
        copy.start()
    expert_in(NS - 1)
    for st in ORDER:
        pl.semaphore_signal(
            free, inc=1, device_id=(grp_partner(g, st), l), device_id_type=MESH
        )
    for copy in back_weights(1):
        copy.start()

    def activate(i, carry):
        h = silu(accg[pl.ds(i * 2, 2)]) * accu[pl.ds(i * 2, 2)]
        hidden[pl.ds(pl.multiple_of(i * PACK, PACK), PACK), :] = h.reshape(PACK, FF).astype(BF16)
        return carry

    lax.fori_loop(0, GRP // 2, activate, 0)

    drain(meta_all.at[pl.ds(0, LOC - 1)], ms)
    drain(wsh.at[pl.ds(0, 3 * SHARD), 0:SH], w_s.at[0])
    drain(wsh.at[pl.ds(0, 3 * SHARD), SH : 2 * SH], w_s.at[1])
    drain(wsh.at[pl.ds(0, 12 * SHARD), 0:SH], w_s.at[3])
    drain(wsh.at[pl.ds(0, 12 * SHARD), SH : 2 * SH], w_s.at[4])

    def sent(s, carry):
        drain(xall.at[s, pl.ds(0, 3)], ag_s.at[s])
        drain(xall.at[s, pl.ds(0, 4)], sib_s.at[s])
        drain(cot_all.at[s, 0, pl.ds(0, 3 * T)], cg_s.at[s])
        drain(cot_all.at[s, 0], cs_s.at[s])
        drain(cot_all.at[s, 0], cs_r.at[s])
        return carry

    lax.fori_loop(0, NS, sent, 0)
    for s_last in range(NS - RING, NS):
        drain(sbuf.at[s_last % RING, pl.ds(0, GRP - 1)], d_s.at[s_last])
    for copy in cotangents(0):
        copy.start()

    def expert_out(s):
        spot, slot_now = s % RING, (s + 1) % 2
        drain(wgb.at[slot_now], hbm.at[0, slot_now])
        if not isinstance(s, int):

            @pl.when(s >= RING)
            def _():
                drain(sbuf.at[spot, pl.ds(0, GRP - 1)], o_s.at[s - RING])

        def rows(i, carry):
            r = pl.ds(pl.multiple_of(i * 4 * CAP, 4 * CAP), 4 * CAP)
            o = dot(hidden[r, 0:W], wgb[slot_now, :, 0:W])
            o = o + dot(hidden[r, W : 2 * W], wgb[slot_now, :, W : 2 * W])
            o = o.reshape(4, CAP, W)
            sbuf[spot, pl.ds(i * 4, 4)] = jnp.concatenate(
                [o[:, :, :HALF], o[:, :, HALF:]], axis=1
            ).astype(BF16)
            return carry

        lax.fori_loop(0, GRP // 4, rows, 0)
        if isinstance(s, int) and s == 0:
            pl.semaphore_wait(free, len(ORDER))
        for st in ORDER:
            p = grp_partner(g, st)
            send(sbuf.at[spot, p], rbuf.at[s, g], o_s.at[s], o_r.at[s], (p, l))
        pltpu.make_async_copy(sbuf.at[spot, g], rbuf.at[s, g], o_l.at[s]).start()

    expert_out(0)
    expert_out(1)
    drain(sda.at[pl.ds(0, D - SHARD)], w_r.at[2])
    drain(sda.at[pl.ds(0, D - SHARD)], w_s.at[2])

    def combine(s):
        slot_now = (s + 1) % 2
        drain(rbuf.at[s, pl.ds(0, GRP - 1)], o_r.at[s])
        drain(rbuf.at[s, 0], o_l.at[s])
        for half in range(2):
            first = 0 if half == 0 else PACK - SUP
            cw = cwa if half == 0 else cwb
            rows_sd = pl.ds(pl.multiple_of(s * W + half * HALF, HALF), HALF)
            cols = slice(half * HALF, (half + 1) * HALF)

            def tokens(i, carry):
                y = rbuf[s, :, first : first + SUP, :].reshape(GRP * SUP, HALF)
                rows = pl.ds(pl.multiple_of(i * 256, 256), 256)
                part = dot(cw[rows, :], y) + dot_nt(shared_hidden[rows, :], sda[rows_sd, :])
                xall[s, pl.ds(i * 2, 2), :, cols] = part.reshape(2, T, HALF).astype(BF16)
                return carry

            lax.fori_loop(0, COL // 256, tokens, 0)
            for dz, dc in LOC_STEPS:
                pl_, blk = loc_partner(z, c, dz, dc)
                send(
                    xall.at[s, blk, :, cols], rrecv.at[s, me, :, cols], p_s.at[s], p_r.at[s],
                    (g, pl_),
                )
        rrecv[s, me] = xall[s, me]

        drain(wub.at[slot_now], hbm.at[1, slot_now])
        for half in range(2):
            first = 0 if half == 0 else PACK - SUP
            shift = 0.0 if half == 0 else float(SUP - CAP)
            cols = slice(half * HALF, (half + 1) * HALF)

            def products(i, carry):
                y = rbuf[s, pl.ds(i * 4, 4), first : first + SUP, :].reshape(4 * SUP, HALF)
                pos = lax.broadcasted_iota(jnp.int32, (SUP, COL // 2), 0).astype(F32) - shift
                for h in range(2):
                    tok = slice(h * COL // 2, (h + 1) * COL // 2)
                    ct = wub[slot_now, :, h * W + half * HALF : h * W + (half + 1) * HALF]
                    prod = dot_nt(y, ct).reshape(4, SUP, COL // 2)
                    sl = slots4[i, :, tok]
                    sums = [
                        jnp.sum(
                            jnp.where(pos == sl[e : e + 1, :], prod[e], 0.0), axis=0, keepdims=True
                        )
                        for e in range(4)
                    ]
                    gacc[i, :, tok] += jnp.concatenate(sums, axis=0)
                return carry

            lax.fori_loop(0, GRP // 4, products, 0)

    def total(s):
        drain(rrecv.at[s, pl.ds(0, LOC - 1)], p_r.at[s])
        acc = rrecv[s, 0].astype(F32)
        for b in range(1, LOC):
            acc = acc + rrecv[s, b].astype(F32)
        out[:, pl.ds(pl.multiple_of(s * W, W), W)] = acc.astype(BF16)

    def back_step(s, carry):
        @pl.when(s + 1 < NS)
        def _():
            for copy in cotangents(s + 1):
                copy.start()

        @pl.when(s + 2 < NS)
        def _():
            for copy in back_weights(s + 2):
                copy.start()

        combine(s)

        @pl.when(s + 2 < NS)
        def _():
            expert_out(s + 2)

        @pl.when(s > 0)
        def _():
            total(s - 1)

        return carry

    lax.fori_loop(0, NS, back_step, 0)

    grads = jnp.zeros((8, COL), F32)
    for i in range(4):
        block = gacc[i]
        for j in range(4):
            e = ((4 * i + j) * LOC + l).astype(F32)
            grads = grads + jnp.where(ids == e, block[j : j + 1, :], 0.0)
    for b in range(LOC):
        ggs[b] = grads[:, b * T : (b + 1) * T]
    for dz, dc in LOC_STEPS:
        pl_, blk = loc_partner(z, c, dz, dc)
        send(ggs.at[blk], ggr.at[me], g_s, g_r, (g, pl_))
    ggr[me] = ggs[me]
    total(NS - 1)
    drain(ggr.at[pl.ds(0, LOC - 1)], g_r)
    acc = ggr[0]
    for b in range(1, LOC):
        acc = acc + ggr[b]
    gg[...] = acc

    drain(ggs.at[pl.ds(0, LOC - 1)], g_s)

    def finish(s, carry):
        drain(xall.at[s, pl.ds(0, LOC - 1)], p_s.at[s])
        return carry

    lax.fori_loop(0, NS, finish, 0)
    for s_last in range(NS - RING, NS):
        drain(sbuf.at[s_last % RING, pl.ds(0, GRP - 1)], o_s.at[s_last])


def results(out, grads, out_copy, grads_copy):
    out_copy[...] = out[...]
    grads_copy[...] = grads[...]


def body(
    stream_in, norm_gain, shared_gate, shared_up, shared_down, expert_gate, expert_up, expert_down,
    expert_ids, gate_weights, cotangent,
):
    vm = pl.BlockSpec(memory_space=pltpu.VMEM)
    hb = pl.BlockSpec(memory_space=pl.ANY)
    dma = pltpu.SemaphoreType.DMA
    out, grads, _ = pl.pallas_call(
        layer_kernel,
        out_shape=(
            jax.ShapeDtypeStruct((T, D), BF16),
            jax.ShapeDtypeStruct((8, T), F32),
            jax.ShapeDtypeStruct((NS, 2, COL // 2, W), BF16),
        ),
        in_specs=[vm] * 8 + [hb] * 3,
        out_specs=(vm, vm, hb),
        scratch_shapes=[
            pltpu.VMEM((NS, LOC, T, W), BF16),
            pltpu.VMEM((GRP * SUP, COL), BF16),
            pltpu.VMEM((RING, GRP, PACK, HALF), BF16),
            pltpu.VMEM((NS, GRP, PACK, HALF), BF16),
            pltpu.VMEM((GRP, CAP, FF), F32),
            pltpu.VMEM((GRP, CAP, FF), F32),
            pltpu.VMEM((2, W, FF), BF16),
            pltpu.VMEM((2, W, FF), BF16),
            pltpu.VMEM((D, 2 * SH), BF16),
            pltpu.VMEM((COL, 2 * SH), F32),
            pltpu.VMEM((LOC, 16, T), F32),
            pltpu.VMEM((GRP * CAP, FF), BF16),
            pltpu.VMEM((COL, SH), BF16),
            pltpu.VMEM((GRP, COL), F32),
            pltpu.VMEM((GRP, COL), F32),
            pltpu.VMEM((D, SH), BF16),
            pltpu.VMEM((COL, GRP * SUP), BF16),
            pltpu.VMEM((COL, GRP * SUP), BF16),
            pltpu.VMEM((4, 4, COL), F32),
            pltpu.VMEM((4, 4, COL), F32),
            pltpu.VMEM((NS, LOC, T, W), BF16),
            pltpu.VMEM((LOC, 8, T), F32),
            pltpu.VMEM((LOC, 8, T), F32),
        ]
        + [dma(())] * 4
        + [pltpu.SemaphoreType.REGULAR]
        + [dma((NS,))] * 17
        + [dma((5,))] * 2
        + [dma((3,))]
        + [dma((2, 2))],
        compiler_params=pltpu.CompilerParams(
            collective_id=0, has_side_effects=True, vmem_limit_bytes=VMEM_LIMIT
        ),
        name="layer",
    )(
        stream_in, norm_gain, expert_ids.T, gate_weights.T, shared_gate, shared_up, shared_down.T,
        cotangent, expert_gate, expert_up, expert_down,
    )
    out, grads = pl.pallas_call(
        results,
        out_shape=(jax.ShapeDtypeStruct((T, D), BF16), jax.ShapeDtypeStruct((8, T), F32)),
        in_specs=[vm, vm],
        out_specs=(vm, vm),
        name="results",
    )(out, grads)
    return out, grads.T


def solution(mesh):
    rows = P(("grp", "loc"), None)
    experts = P(("grp", "loc"), None, None)
    return jax.shard_map(
        body,
        mesh=mesh,
        in_specs=(
            rows, P(), P("grp", "loc"), P("grp", "loc"), P("loc", "grp"), experts, experts, experts,
            rows, rows, rows,
        ),
        out_specs=(rows, rows),
        check_vma=False,
    )
```
